256 devices in a mesh: lat: 64 (over x, z, core), fld: 4 (over y).
Axes of the slice: x: 4, y: 4, z: 8, core: 2. Of those that a mesh axis runs over, the one named last changes fastest.
Arguments:
- fourier: bfloat16 [2, 2560, 16, 2, 1280], P(None, 'lat', 'fld'), may hold values from -6 to 6
- legendre: bfloat16 [819840, 1280], P('lat', 'fld'), may hold values from -0.125 to 0.125
- cycle_points: int32 [2560], P('lat'), may hold values from 8 to 5136, as said below
- wave_order: int32 [1280], replicated, may hold values from 0 to 1279, as said below
Outputs:
- spectral: float32 [2, 32, 819840], P(None, 'fld', 'lat')
The draws below stay inside these ranges and needn't reach their ends.
Inputs may be any that keep to these rules, and one draw needn't show every extreme that they name: `cycle_points`: rows r and r + 1280 hold the same count; for r < 1280 the count is 20 + 4 r minus 0, 4, 8 or 12; row 0 holds 8 and row 1279 holds 5136. `wave_order`: every wavenumber appears once; entries 2 k and 2 k + 1 are a wavenumber below 640 and 1279 minus it.
All inputs are finite; a program needn't handle non-finite values.
Results may differ from the reference program's by a relative error of at most 0.0031.
Values may be sent and summed in bfloat16 or wider, within the bound.
A program may use at most 128 MiB of HBM per device.

```python
import jax
import jax.numpy as jnp
from jax import lax

NLAT = 2560
MW = 1280
FB = 16
BATCHES = 2
NH = 1280
MPL = 20
ROWS_OWN = 12810
ROWS_ALL = 819840
N_LAT = 64


def draw_cycle_points(key, part):
    cycle_index = jnp.arange(NH, dtype=jnp.int32)
    cycle_trim = jax.random.randint(key, (NH,), 0, 4, dtype=jnp.int32)
    cycle_trim = jnp.where(cycle_index == NH - 1, 0, cycle_trim)
    cycle_trim = jnp.where(cycle_index == 0, 3, cycle_trim)
    counts = 20 + 4 * cycle_index - 4 * cycle_trim
    return jnp.concatenate([counts, counts]).astype(jnp.int32)


def draw_wave_order(key, part):
    low_waves = jax.random.permutation(key, MW // 2).astype(jnp.int32)
    return jnp.stack([low_waves, MW - 1 - low_waves], axis=1).reshape(MW).astype(jnp.int32)


def shard_levels(rng, dims, pieces, smallest, high):
    factor_of, own = 1.0, jax.random.fold_in(rng, 6)
    for dim, parts in pieces:
        heights = jnp.exp(jax.random.uniform(jax.random.fold_in(own, dim), (parts,), jnp.float32, smallest / len(pieces), high / len(pieces)))
        factor_of = factor_of * jnp.repeat(heights, dims[dim] // parts).reshape([-1 if axis == dim else 1 for axis in range(len(dims))])
    return factor_of


def bell_draw(own_key, extent, width, reach, cuts=(), kind=jnp.bfloat16):
    array = jax.random.normal(own_key, extent, jnp.float32) * width
    if len(cuts) > 0:
        array = shard_levels(own_key, extent, cuts, -0.22, 0.18) * array
    return jnp.clip(array, min=-reach, max=reach).astype(kind)


def setup_inputs(seed: int = 0) -> dict:
    arg_keys = jax.random.split(jax.random.key(seed), 5)
    fourier = bell_draw(arg_keys[0], (BATCHES, NLAT, FB, 2, MW), 1.0, 6.0, ((1, 64), (2, 4)))
    legendre = bell_draw(arg_keys[1], (ROWS_ALL, NH), NLAT ** -0.5, 0.125, ((0, 64), (1, 4)))
    cycle_points = draw_cycle_points(jax.random.fold_in(arg_keys[4], 71), 0)
    wave_order = draw_wave_order(jax.random.fold_in(arg_keys[4], 71), 0)
    return {"fourier": fourier, "legendre": legendre, "cycle_points": cycle_points, "wave_order": wave_order}


def select_rows(product, first_count, row_total):
    pair_count = product.shape[0]
    col_width = product.shape[2] // 2
    halves = product.reshape(pair_count, row_total, 2, col_width)
    first_mask = jnp.arange(row_total, dtype=jnp.int32)[None, :] < first_count[:, None]
    return jnp.where(first_mask[:, :, None], halves[:, :, 0], halves[:, :, 1])


def arrange(data_block, pair_count):
    batch_size = data_block.shape[0]
    lat_depth = data_block.shape[1]
    fields = data_block.shape[2]
    shaped = data_block.reshape(batch_size, lat_depth, fields, 2, pair_count, 2)
    shaped = jnp.transpose(shaped, (4, 1, 5, 0, 2, 3))
    return shaped.reshape(pair_count, lat_depth, 4 * batch_size * fields)


def owner_rows(by_wave, legendre, wave_limit, wave_order, owner_index):
    owned_waves = lax.dynamic_slice_in_dim(wave_order, owner_index * MPL, MPL)
    tables = lax.dynamic_slice_in_dim(legendre, owner_index * ROWS_OWN, ROWS_OWN, 0)
    picked = jnp.take(by_wave, owned_waves, axis=0)
    picked = jnp.moveaxis(picked, 0, 4)
    keep_mask = owned_waves[None, :] < wave_limit[:, None]
    picked = jnp.where(keep_mask[None, :, None, None, :], picked, jnp.zeros((), picked.dtype))
    north_rows = picked[:, :NH].astype(jnp.float32)
    south_rows = picked[:, NH:].astype(jnp.float32)
    sym_rows = (north_rows + south_rows).astype(jnp.bfloat16)
    anti_rows = (north_rows - south_rows).astype(jnp.bfloat16)
    pair_count = MPL // 2
    even_rows = MW // 2 + 1
    tables = tables.reshape(pair_count, MW + 1, NH).astype(jnp.float32)
    even_part = jnp.einsum("prk,pkn->prn", tables[:, :even_rows], arrange(sym_rows, pair_count).astype(jnp.float32), precision=lax.Precision.HIGHEST)
    odd_part = jnp.einsum("prk,pkn->prn", tables[:, even_rows:], arrange(anti_rows, pair_count).astype(jnp.float32), precision=lax.Precision.HIGHEST)
    degree_count = MW - owned_waves[0::2]
    even_part = select_rows(even_part, (degree_count + 1) // 2, even_rows)
    odd_part = select_rows(odd_part, degree_count // 2, MW // 2)
    return jnp.concatenate([even_part, odd_part], axis=1).reshape(ROWS_OWN, -1)


def reference(fourier, legendre, cycle_points, wave_order):
    wave_limit = jnp.minimum(cycle_points // 2, MW)
    by_wave = jnp.moveaxis(fourier, 4, 0)

    def one_owner(owner_index):
        return owner_rows(by_wave, legendre, wave_limit, wave_order, owner_index)

    blocks = lax.map(one_owner, jnp.arange(N_LAT, dtype=jnp.int32))
    blocks = blocks.reshape(N_LAT * ROWS_OWN, BATCHES, 2 * FB)
    return jnp.transpose(blocks, (1, 2, 0))
```

```python
import functools

import jax
import jax.numpy as jnp
from jax import lax
from jax.experimental import pallas as pl
from jax.experimental.pallas import tpu as pltpu
from jax.sharding import PartitionSpec as P

MESH = pl.DeviceIdType.MESH
NT = (((1,), (1,)), ((), ()))
ROW_PAD = 24


def round_up(value, step):
    return -(-value // step) * step


def exchange_kernel(
    n_lat,
    n_fld,
    lane_tile,
    x_ref,
    waves_ref,
    limit_ref,
    owned_ref,
    legendre_ref,
    out_ref,
    send_buf,
    recv_buf,
    tables,
    mixed_sym,
    mixed_anti,
    rows_sym,
    rows_anti,
    partial,
    part_send,
    part_recv,
    send_sem,
    recv_sem,
    table_sem,
    part_send_sem,
    part_recv_sem,
):
    lat = lax.axis_index("lat")
    fld = lax.axis_index("fld")
    half = n_lat // 2
    depth = half // n_fld
    hemi = lat // half
    block = (lat % half) // depth
    place = lat % depth
    owner_waves, columns = send_buf.shape[1], send_buf.shape[2]
    wave_count = x_ref.shape[1]
    kinds = part_send.shape[1]
    rows_each = columns // kinds
    pairs = owner_waves // 2
    own = block == fld
    lat_depth, total = legendre_ref.shape

    load = pltpu.make_async_copy(legendre_ref, tables, table_sem)
    load.start()

    barrier = pltpu.get_barrier_semaphore()

    def greet(s, carry):
        source_fld = s // (2 * depth)
        rest = s % (2 * depth)
        source_lat = (rest // depth) * half + fld * depth + rest % depth
        itself = jnp.logical_and(source_lat == lat, source_fld == fld)

        @pl.when(jnp.logical_not(itself))
        def _():
            pl.semaphore_signal(
                barrier, inc=1, device_id=(source_lat, source_fld), device_id_type=MESH
            )

        return carry

    lax.fori_loop(0, n_fld * 2 * depth, greet, 0)
    for d in range(1, n_fld):
        pl.semaphore_signal(
            barrier, inc=1, device_id=(lat, (fld + d) % n_fld), device_id_type=MESH
        )

    slot = (fld * 2 + hemi) * depth + place

    def copy_to(owner):
        return pltpu.make_async_remote_copy(
            src_ref=send_buf.at[owner],
            dst_ref=recv_buf.at[slot],
            send_sem=send_sem.at[owner],
            recv_sem=recv_sem.at[slot],
            device_id=(owner, block),
            device_id_type=MESH,
        )

    group = min(8, n_lat)
    groups = n_lat // group
    lane = lax.broadcasted_iota(jnp.int32, (group * ROW_PAD, 128), 1)

    def reorder(step):
        number = (lat // group + step) % groups
        start = pl.multiple_of(number * (group * ROW_PAD), group * ROW_PAD)
        wave = waves_ref[pl.ds(start, group * ROW_PAD), :]
        pieces = []
        for v in range(-(-wave_count // 128)):
            width = min(128, wave_count - 128 * v)
            hit = jnp.where(wave == lane + 128 * v, 1.0, 0.0).astype(jnp.bfloat16)
            pieces.append(hit[:, :width])
        chosen = jnp.concatenate(pieces, axis=1)
        picked = lax.dot_general(
            chosen, x_ref[...], NT, preferred_element_type=jnp.float32
        )
        wide = jnp.concatenate([wave] * (-(-columns // 128)), axis=1)[:, :columns]
        picked = jnp.where(wide < limit_ref[...], picked, 0.0)
        for o in range(group):
            part = picked[o * ROW_PAD : o * ROW_PAD + owner_waves]
            send_buf[number * group + o] = part.astype(jnp.bfloat16)
        return number

    def send(number):
        def one(o, carry):
            owner = number * group + (lat + o) % group
            itself = jnp.logical_and(own, owner == lat)

            @pl.when(itself)
            def _():
                pltpu.make_async_copy(
                    send_buf.at[owner], recv_buf.at[slot], recv_sem.at[slot]
                ).start()

            @pl.when(jnp.logical_not(itself))
            def _():
                copy_to(owner).start()

            return carry

        lax.fori_loop(0, group, one, 0)

    number = reorder(0)
    pl.semaphore_wait(barrier, n_lat + n_fld - 1 - own.astype(jnp.int32))
    send(number)

    def sender(step, carry):
        send(reorder(step))
        return carry

    lax.fori_loop(1, groups, sender, 0)
    load.wait()

    def arrived(s, carry):
        pltpu.make_async_copy(recv_buf.at[s], recv_buf.at[s], recv_sem.at[s]).wait()
        return carry

    lax.fori_loop(0, n_fld * 2 * depth, arrived, 0)

    def gather_field(f, carry):
        for a in range(depth):
            north = recv_buf[(2 * f) * depth + a].astype(jnp.float32)
            south = recv_buf[(2 * f + 1) * depth + a].astype(jnp.float32)
            mixed_sym[a] = north + south
            mixed_anti[a] = north - south
        for mixed, rows in ((mixed_sym, rows_sym), (mixed_anti, rows_anti)):
            for k in range(kinds):
                lo = k * rows_each
                joined = jnp.concatenate(
                    [mixed[a, :, lo : lo + rows_each] for a in range(depth)], axis=1
                )
                for v in range(-(-lat_depth // 128)):
                    width = min(128, lat_depth - 128 * v)
                    rows[
                        v,
                        pl.ds(f * kinds + k, owner_waves, stride=n_fld * kinds),
                        0:width,
                    ] = joined[:, 128 * v : 128 * v + width]
        return carry

    lax.fori_loop(0, n_fld, gather_field, 0)

    per_wave = n_fld * kinds
    even = wave_count // 2 + 1
    sym_end = round_up(even + pairs, lane_tile)
    anti_start = even // lane_tile * lane_tile

    def operand(rows, pair):
        start = pl.multiple_of(pair * (2 * per_wave), 2 * per_wave)
        parts = []
        for v in range(-(-lat_depth // 128)):
            width = min(128, lat_depth - 128 * v)
            parts.append(rows[v, pl.ds(start, 2 * per_wave), 0:width])
        return jnp.concatenate(parts, axis=1).astype(jnp.bfloat16)

    def project(left, start, width):
        return jnp.dot(left, tables[:, pl.ds(start, width)], preferred_element_type=jnp.float32)

    def choose(product, first):
        return jnp.where(first, product[:per_wave], product[per_wave:])

    def degree_index(width, offset):
        return lax.broadcasted_iota(jnp.int32, (per_wave, width), 1) + offset

    def part_copy(d, lo, width, number):
        peer = (fld + d) % n_fld
        return pltpu.make_async_remote_copy(
            src_ref=part_send.at[peer, :, pl.ds(lo, width)],
            dst_ref=part_recv.at[d - 1, :, pl.ds(lo, width)],
            send_sem=part_send_sem.at[d - 1, number],
            recv_sem=part_recv_sem.at[d - 1, number],
            device_id=(lat, peer),
            device_id_type=MESH,
        )

    def left_over(pair, start, width):
        first_rows = lax.shift_right_logical(wave_count - owned_ref[2 * pair], 1)
        product = project(operand(rows_anti, pair), start, width)
        degree = degree_index(width, 0) + (wave_count // 2 - 1 - pair)
        return choose(product, degree < first_rows)

    def pair_chunk(c, carry):
        start = pl.multiple_of(c * wave_count, min(wave_count, 1280))
        wave = owned_ref[2 * c]
        first_even = lax.shift_right_logical(wave_count + 1 - wave, 1)
        first_odd = lax.shift_right_logical(wave_count - wave, 1)
        sym = project(operand(rows_sym, c), start, sym_end)
        sym = choose(sym, degree_index(sym_end, -c) < first_even)
        anti_width = wave_count - anti_start
        anti_from = pl.multiple_of(start + anti_start, lane_tile)
        anti = project(operand(rows_anti, c), anti_from, anti_width)
        anti = choose(anti, degree_index(anti_width, anti_start - even - c) < first_odd)
        before = left_over(jnp.maximum(c - 1, 0), start, lane_tile)
        head = jnp.where(degree_index(lane_tile, 0) < c, before, sym[:, :lane_tile])
        middle = jnp.where(
            degree_index(sym_end - anti_start, anti_start - c) < even,
            sym[:, anti_start:],
            anti[:, : sym_end - anti_start],
        )
        pieces = [head, sym[:, lane_tile:anti_start], middle, anti[:, sym_end - anti_start :]]
        at = 0
        for piece in pieces:
            width = piece.shape[1]
            if width == 0:
                continue
            lanes = pl.ds(pl.multiple_of(start + at, lane_tile), width)
            partial[:, lanes] = piece
            for f in range(n_fld):
                part_send[f, :, lanes] = piece[f * kinds : (f + 1) * kinds].astype(jnp.bfloat16)
            at += width
        for d in range(1, n_fld):
            part_copy(d, start, wave_count, c).start()
        return carry

    lax.fori_loop(0, pairs, pair_chunk, 0)

    tail = total - pairs * wave_count
    tail_from = pairs * wave_count
    piece = left_over(pairs - 1, tail_from, tail)
    partial[:, tail_from : tail_from + tail] = piece
    for f in range(n_fld):
        part_send[f, :, tail_from : tail_from + tail] = piece[
            f * kinds : (f + 1) * kinds
        ].astype(jnp.bfloat16)
    tail_wide = part_send.shape[2] - tail_from
    for d in range(1, n_fld):
        part_copy(d, tail_from, tail_wide, pairs).start()

    mine = pl.multiple_of(fld * kinds, kinds)
    batch_rows = kinds // 2

    def finish(lo, width, kept, number):
        for d in range(1, n_fld):
            part_copy(d, lo, width, number).wait_recv()
        result = partial[pl.ds(mine, kinds), pl.ds(lo, kept)]
        for d in range(1, n_fld):
            result = result + part_recv[d - 1, :, pl.ds(lo, kept)].astype(jnp.float32)
        out_ref[0, :, pl.ds(lo, kept)] = result[:batch_rows]
        out_ref[1, :, pl.ds(lo, kept)] = result[batch_rows:]

    def finish_pair(c, carry):
        start = pl.multiple_of(c * wave_count, min(wave_count, 1280))
        finish(start, wave_count, wave_count, c)
        return carry

    lax.fori_loop(0, pairs, finish_pair, 0)
    finish(tail_from, tail_wide, tail, pairs)

    def sent(owner, carry):
        @pl.when(jnp.logical_not(jnp.logical_and(own, owner == lat)))
        def _():
            copy_to(owner).wait_send()

        return carry

    lax.fori_loop(0, n_lat, sent, 0)

    def part_sent(c, carry):
        start = pl.multiple_of(c * wave_count, min(wave_count, 1280))
        for d in range(1, n_fld):
            part_copy(d, start, wave_count, c).wait_send()
        return carry

    lax.fori_loop(0, pairs, part_sent, 0)
    for d in range(1, n_fld):
        part_copy(d, tail_from, tail_wide, pairs).wait_send()


def shards(fourier, legendre, cycle_points, wave_order, lane_tile=256):
    n_lat, n_fld = lax.axis_size("lat"), lax.axis_size("fld")
    batches, rows_each, fields, parts, wave_count = fourier.shape
    kinds = batches * fields * parts
    columns = kinds * rows_each
    owner_waves = wave_count // n_lat
    total, lat_depth = legendre.shape
    depth = n_lat // 2 // n_fld
    per_wave = n_fld * kinds
    padded = round_up(total, 128)
    tiles = -(-lat_depth // 128)

    x = jnp.transpose(fourier, (0, 2, 3, 1, 4)).reshape(columns, wave_count)
    waves = jnp.pad(
        wave_order.reshape(n_lat, owner_waves),
        ((0, 0), (0, ROW_PAD - owner_waves)),
        constant_values=-1,
    ).reshape(n_lat * ROW_PAD, 1)
    waves = jnp.broadcast_to(waves, (n_lat * ROW_PAD, 128))
    limit = jnp.tile(jnp.minimum(cycle_points // 2, wave_count), kinds).reshape(1, columns)
    owned = lax.dynamic_slice_in_dim(
        wave_order, lax.axis_index("lat") * owner_waves, owner_waves
    )
    vmem = pl.BlockSpec(memory_space=pltpu.VMEM)
    return pl.pallas_call(
        functools.partial(exchange_kernel, n_lat, n_fld, lane_tile),
        out_shape=jax.ShapeDtypeStruct((batches, fields * parts, total), jnp.float32),
        in_specs=[
            vmem,
            vmem,
            vmem,
            pl.BlockSpec(memory_space=pltpu.SMEM),
            pl.BlockSpec(memory_space=pl.ANY),
        ],
        out_specs=vmem,
        scratch_shapes=[
            pltpu.VMEM((n_lat, owner_waves, columns), jnp.bfloat16),
            pltpu.VMEM((2 * depth * n_fld, owner_waves, columns), jnp.bfloat16),
            pltpu.VMEM((lat_depth, total), jnp.bfloat16),
            pltpu.VMEM((depth, owner_waves, columns), jnp.float32),
            pltpu.VMEM((depth, owner_waves, columns), jnp.float32),
            pltpu.VMEM((tiles, owner_waves * per_wave, 128), jnp.float32),
            pltpu.VMEM((tiles, owner_waves * per_wave, 128), jnp.float32),
            pltpu.VMEM((per_wave, padded), jnp.float32),
            pltpu.VMEM((n_fld, kinds, padded), jnp.bfloat16),
            pltpu.VMEM((n_fld - 1, kinds, padded), jnp.bfloat16),
            pltpu.SemaphoreType.DMA((n_lat,)),
            pltpu.SemaphoreType.DMA((2 * depth * n_fld,)),
            pltpu.SemaphoreType.DMA,
            pltpu.SemaphoreType.DMA((n_fld - 1, owner_waves // 2 + 1)),
            pltpu.SemaphoreType.DMA((n_fld - 1, owner_waves // 2 + 1)),
        ],
        compiler_params=pltpu.CompilerParams(
            collective_id=0, has_side_effects=True, vmem_limit_bytes=56 * 2**20
        ),
        cost_estimate=pl.CostEstimate(
            flops=4 * columns * wave_count * wave_count,
            bytes_accessed=total * lat_depth * 2,
            transcendentals=0,
        ),
    )(x, waves, limit, owned, legendre.T)


def solution(mesh):
    placed = (P(None, "lat", "fld", None, None), P("lat", "fld"), P("lat"), P())
    return jax.shard_map(
        shards, mesh=mesh, in_specs=placed, out_specs=P(None, "fld", "lat"), check_vma=False
    )
```

```python
import functools

import jax
import jax.numpy as jnp
from jax import lax
from jax.experimental import pallas as pl
from jax.experimental.pallas import tpu as pltpu
from jax.sharding import PartitionSpec as P

MESH = pl.DeviceIdType.MESH
NT = (((1,), (1,)), ((), ()))


def round_up(value, step):
    return -(-value // step) * step


def exchange_kernel(
    n_lat,
    n_fld,
    lane_tile,
    sizes,
    x_ref,
    waves_ref,
    owned_ref,
    legendre_ref,
    out_ref,
    *scratch,
):
    n_groups = len(sizes)
    send_bufs, scratch = scratch[:n_groups], scratch[n_groups:]
    recv_bufs, scratch = scratch[:n_groups], scratch[n_groups:]
    (
        wave_cols,
        tables,
        mixed_sym,
        mixed_anti,
        rows_sym,
        rows_anti,
        partial,
        part_send,
        part_recv,
        send_sem,
        recv_sem,
        table_sem,
        part_send_sem,
        part_recv_sem,
    ) = scratch
    lat = lax.axis_index("lat")
    fld = lax.axis_index("fld")
    half = n_lat // 2
    depth = half // n_fld
    sources = 2 * depth
    hemi = lat // half
    block = (lat % half) // depth
    place = lat % depth
    columns, wave_count = x_ref.shape
    owner_waves = sum(sizes)
    kinds = part_send.shape[1]
    rows_each = columns // kinds
    pairs = owner_waves // 2
    own = block == fld
    lat_depth, total = legendre_ref.shape
    first_owned = lat * owner_waves

    load = pltpu.make_async_copy(legendre_ref, tables, table_sem)
    load.start()

    barrier = pltpu.get_barrier_semaphore()

    def greet(s, carry):
        source_fld = s // sources
        rest = s % sources
        source_lat = (rest // depth) * half + fld * depth + rest % depth
        itself = jnp.logical_and(source_lat == lat, source_fld == fld)

        @pl.when(jnp.logical_not(itself))
        def _():
            pl.semaphore_signal(
                barrier, inc=1, device_id=(source_lat, source_fld), device_id_type=MESH
            )

        return carry

    lax.fori_loop(0, n_fld * sources, greet, 0)
    for d in range(1, n_fld):
        pl.semaphore_signal(
            barrier, inc=1, device_id=(lat, (fld + d) % n_fld), device_id_type=MESH
        )

    slot = fld * sources + hemi * depth + place

    def copy_to(number, owner):
        return pltpu.make_async_remote_copy(
            src_ref=send_bufs[number].at[owner],
            dst_ref=recv_bufs[number].at[slot],
            send_sem=send_sem.at[number, owner],
            recv_sem=recv_sem.at[number, slot],
            device_id=(owner, block),
            device_id_type=MESH,
        )

    for v in range(-(-wave_count // 128)):
        width = min(128, wave_count - 128 * v)
        line = waves_ref[:, 128 * v : 128 * v + width]
        wave_cols[128 * v : 128 * v + width] = jnp.broadcast_to(line, (128, width)).T

    wave_cols[wave_count : wave_count + 8] = jnp.full((8, 128), -1, jnp.int32)

    lane = lax.broadcasted_iota(jnp.int32, (n_lat * 8, 128), 1)

    def reorder(number):
        first = 8 * number
        wave = jnp.concatenate(
            [wave_cols[o * owner_waves + first : o * owner_waves + first + 8] for o in range(n_lat)],
            axis=0,
        )
        pieces = []
        for v in range(-(-wave_count // 128)):
            width = min(128, wave_count - 128 * v)
            hit = jnp.where(wave == lane + 128 * v, 1.0, 0.0).astype(jnp.bfloat16)
            pieces.append(hit[:, :width])
        chosen = jnp.concatenate(pieces, axis=1)
        picked = lax.dot_general(
            chosen, x_ref[...], NT, preferred_element_type=jnp.float32
        )
        for o in range(n_lat):
            part = picked[8 * o : 8 * o + sizes[number]]
            send_bufs[number][o] = part.astype(jnp.bfloat16)

    def send(number):
        def several(u, carry):
            for n in range(8):
                if n_lat == 64:
                    owner = (
                        (lat // 16 + u % 4 + n) % 4 * 16
                        + (lat // 2 % 8 + (4, 1, 7, 2, 6, 3, 5, 0)[n]) % 8 * 2
                        + (lat + u // 4 + n) % 2
                    )
                else:
                    owner = (lat + u * 8 + n) % n_lat
                itself = jnp.logical_and(own, owner == lat)

                @pl.when(itself)
                def _():
                    pltpu.make_async_copy(
                        send_bufs[number].at[owner],
                        recv_bufs[number].at[slot],
                        recv_sem.at[number, slot],
                    ).start()

                @pl.when(jnp.logical_not(itself))
                def _():
                    copy_to(number, owner).start()

            return carry

        lax.fori_loop(0, n_lat // 8, several, 0)

    for number in range(n_groups):
        reorder(number)
        if number == 0:
            pl.semaphore_wait(barrier, n_lat + n_fld - 1 - own.astype(jnp.int32))
        send(number)

    def gather_group(number):
        count = sizes[number]
        recv_buf = recv_bufs[number]

        def gather_field(f, carry):
            def arrived(s, carry):
                at = f * sources + s
                pltpu.make_async_copy(
                    recv_buf.at[at], recv_buf.at[at], recv_sem.at[number, at]
                ).wait()
                return carry

            lax.fori_loop(0, sources, arrived, 0)
            for a in range(depth):
                north = recv_buf[f * sources + a].astype(jnp.float32)
                south = recv_buf[f * sources + depth + a].astype(jnp.float32)
                mixed_sym[a, 0:count] = north + south
                mixed_anti[a, 0:count] = north - south
            for mixed, rows in ((mixed_sym, rows_sym), (mixed_anti, rows_anti)):
                for k in range(kinds):
                    lo = k * rows_each
                    joined = jnp.concatenate(
                        [mixed[a, 0:count, lo : lo + rows_each] for a in range(depth)], axis=1
                    )
                    start = 8 * number * n_fld * kinds + f * kinds + k
                    for v in range(-(-lat_depth // 128)):
                        width = min(128, lat_depth - 128 * v)
                        rows[v, pl.ds(start, count, stride=n_fld * kinds), 0:width] = joined[
                            :, 128 * v : 128 * v + width
                        ]
            return carry

        lax.fori_loop(0, n_fld, gather_field, 0)

    per_wave = n_fld * kinds
    even = wave_count // 2 + 1
    sym_end = round_up(even + pairs, lane_tile)
    anti_start = even // lane_tile * lane_tile

    def operand(rows, pair):
        start = pl.multiple_of(pair * (2 * per_wave), 2 * per_wave)
        parts = []
        for v in range(-(-lat_depth // 128)):
            width = min(128, lat_depth - 128 * v)
            parts.append(rows[v, pl.ds(start, 2 * per_wave), 0:width])
        return jnp.concatenate(parts, axis=1).astype(jnp.bfloat16)

    def project(left, start, width):
        return jnp.dot(left, tables[:, pl.ds(start, width)], preferred_element_type=jnp.float32)

    def choose(product, first):
        return jnp.where(first, product[:per_wave], product[per_wave:])

    def degree_index(width, offset):
        return lax.broadcasted_iota(jnp.int32, (per_wave, width), 1) + offset

    def part_copy(d, lo, width, number):
        peer = (fld + d) % n_fld
        return pltpu.make_async_remote_copy(
            src_ref=part_send.at[peer, :, pl.ds(lo, width)],
            dst_ref=part_recv.at[d - 1, :, pl.ds(lo, width)],
            send_sem=part_send_sem.at[d - 1, number],
            recv_sem=part_recv_sem.at[d - 1, number],
            device_id=(lat, peer),
            device_id_type=MESH,
        )

    def left_over(pair, start, width):
        first_rows = lax.shift_right_logical(wave_count - owned_ref[first_owned + 2 * pair], 1)
        product = project(operand(rows_anti, pair), start, width)
        degree = degree_index(width, 0) + (wave_count // 2 - 1 - pair)
        return choose(product, degree < first_rows)

    def pair_chunk(c, carry):
        start = pl.multiple_of(c * wave_count, min(wave_count, 1280))
        wave = owned_ref[first_owned + 2 * c]
        first_even = lax.shift_right_logical(wave_count + 1 - wave, 1)
        first_odd = lax.shift_right_logical(wave_count - wave, 1)
        sym = project(operand(rows_sym, c), start, sym_end)
        sym = choose(sym, degree_index(sym_end, -c) < first_even)
        anti_width = wave_count - anti_start
        anti_from = pl.multiple_of(start + anti_start, lane_tile)
        anti = project(operand(rows_anti, c), anti_from, anti_width)
        anti = choose(anti, degree_index(anti_width, anti_start - even - c) < first_odd)
        before = left_over(jnp.maximum(c - 1, 0), start, lane_tile)
        head = jnp.where(degree_index(lane_tile, 0) < c, before, sym[:, :lane_tile])
        middle = jnp.where(
            degree_index(sym_end - anti_start, anti_start - c) < even,
            sym[:, anti_start:],
            anti[:, : sym_end - anti_start],
        )
        pieces = [head, sym[:, lane_tile:anti_start], middle, anti[:, sym_end - anti_start :]]
        at = 0
        for piece in pieces:
            width = piece.shape[1]
            if width == 0:
                continue
            lanes = pl.ds(pl.multiple_of(start + at, lane_tile), width)
            partial[:, lanes] = piece
            for f in range(n_fld):
                part_send[f, :, lanes] = piece[f * kinds : (f + 1) * kinds].astype(jnp.bfloat16)
            at += width
        for d in range(1, n_fld):
            part_copy(d, start, wave_count, c).start()
        return carry

    tail = total - pairs * wave_count
    tail_from = pairs * wave_count
    tail_wide = part_send.shape[2] - tail_from

    mine = pl.multiple_of(fld * kinds, kinds)
    batch_rows = kinds // 2

    def finish(lo, width, kept, number):
        for d in range(1, n_fld):
            part_copy(d, lo, width, number).wait_recv()
        result = partial[pl.ds(mine, kinds), pl.ds(lo, kept)]
        for d in range(1, n_fld):
            result = result + part_recv[d - 1, :, pl.ds(lo, kept)].astype(jnp.float32)
        out_ref[0, :, pl.ds(lo, kept)] = result[:batch_rows]
        out_ref[1, :, pl.ds(lo, kept)] = result[batch_rows:]

    def finish_pair(c, carry):
        start = pl.multiple_of(c * wave_count, min(wave_count, 1280))
        finish(start, wave_count, wave_count, c)
        return carry

    load.wait()
    finished = 0
    for number in range(n_groups):
        gather_group(number)
        first = 4 * number
        lax.fori_loop(first, first + sizes[number] // 2, pair_chunk, 0)
        if number == n_groups - 2:
            finished = 4 * number
            lax.fori_loop(0, finished, finish_pair, 0)

    piece = left_over(pairs - 1, tail_from, tail)
    partial[:, tail_from : tail_from + tail] = piece
    for f in range(n_fld):
        part_send[f, :, tail_from : tail_from + tail] = piece[
            f * kinds : (f + 1) * kinds
        ].astype(jnp.bfloat16)
    for d in range(1, n_fld):
        part_copy(d, tail_from, tail_wide, pairs).start()

    lax.fori_loop(finished, pairs, finish_pair, 0)
    finish(tail_from, tail_wide, tail, pairs)

    for number in range(n_groups):

        def sent(owner, carry):
            @pl.when(jnp.logical_not(jnp.logical_and(own, owner == lat)))
            def _():
                copy_to(number, owner).wait_send()

            return carry

        lax.fori_loop(0, n_lat, sent, 0)

    def part_sent(c, carry):
        start = pl.multiple_of(c * wave_count, min(wave_count, 1280))
        for d in range(1, n_fld):
            part_copy(d, start, wave_count, c).wait_send()
        return carry

    lax.fori_loop(0, pairs, part_sent, 0)
    for d in range(1, n_fld):
        part_copy(d, tail_from, tail_wide, pairs).wait_send()


def shards(fourier, legendre, cycle_points, wave_order, lane_tile=256):
    n_lat, n_fld = lax.axis_size("lat"), lax.axis_size("fld")
    batches, rows_each, fields, parts, wave_count = fourier.shape
    kinds = batches * fields * parts
    columns = kinds * rows_each
    owner_waves = wave_count // n_lat
    total, lat_depth = legendre.shape
    depth = n_lat // 2 // n_fld
    slots = 2 * depth * n_fld
    per_wave = n_fld * kinds
    padded = round_up(total, 128)
    tiles = -(-lat_depth // 128)

    sizes = tuple(min(8, owner_waves - t) for t in range(0, owner_waves, 8))
    wave_limit = jnp.minimum(cycle_points // 2, wave_count)
    keep_mask = jnp.arange(wave_count, dtype=jnp.int32)[None, :] < wave_limit[:, None]
    kept = jnp.where(keep_mask[None, :, None, None, :], fourier, jnp.zeros((), fourier.dtype))
    x = jnp.transpose(kept, (0, 2, 3, 1, 4)).reshape(columns, wave_count)
    vmem = pl.BlockSpec(memory_space=pltpu.VMEM)
    return pl.pallas_call(
        functools.partial(exchange_kernel, n_lat, n_fld, lane_tile, sizes),
        out_shape=jax.ShapeDtypeStruct((batches, fields * parts, total), jnp.float32),
        in_specs=[
            vmem,
            vmem,
            pl.BlockSpec(memory_space=pltpu.SMEM),
            pl.BlockSpec(memory_space=pl.ANY),
        ],
        out_specs=vmem,
        scratch_shapes=[
            *(pltpu.VMEM((n_lat, count, columns), jnp.bfloat16) for count in sizes),
            *(pltpu.VMEM((slots, count, columns), jnp.bfloat16) for count in sizes),
            pltpu.VMEM((round_up(wave_count, 128) + 8, 128), jnp.int32),
            pltpu.VMEM((lat_depth, total), jnp.bfloat16),
            pltpu.VMEM((depth, 8, columns), jnp.float32),
            pltpu.VMEM((depth, 8, columns), jnp.float32),
            pltpu.VMEM((tiles, owner_waves * per_wave, 128), jnp.float32),
            pltpu.VMEM((tiles, owner_waves * per_wave, 128), jnp.float32),
            pltpu.VMEM((per_wave, padded), jnp.float32),
            pltpu.VMEM((n_fld, kinds, padded), jnp.bfloat16),
            pltpu.VMEM((n_fld - 1, kinds, padded), jnp.bfloat16),
            pltpu.SemaphoreType.DMA((len(sizes), n_lat)),
            pltpu.SemaphoreType.DMA((len(sizes), slots)),
            pltpu.SemaphoreType.DMA,
            pltpu.SemaphoreType.DMA((n_fld - 1, owner_waves // 2 + 1)),
            pltpu.SemaphoreType.DMA((n_fld - 1, owner_waves // 2 + 1)),
        ],
        compiler_params=pltpu.CompilerParams(
            collective_id=0, has_side_effects=True, vmem_limit_bytes=56 * 2**20
        ),
        cost_estimate=pl.CostEstimate(
            flops=4 * columns * wave_count * wave_count,
            bytes_accessed=total * lat_depth * 2,
            transcendentals=0,
        ),
    )(x, wave_order.reshape(1, wave_count), wave_order, legendre.T)


def solution(mesh):
    placed = (P(None, "lat", "fld", None, None), P("lat", "fld"), P("lat"), P())
    return jax.shard_map(
        shards, mesh=mesh, in_specs=placed, out_specs=P(None, "fld", "lat"), check_vma=False
    )
```

```python
import functools

import jax
import jax.numpy as jnp
from jax import lax
from jax.experimental import pallas as pl
from jax.experimental.pallas import tpu as pltpu
from jax.sharding import PartitionSpec as P

MESH = pl.DeviceIdType.MESH
NT = (((1,), (1,)), ((), ()))


def round_up(value, step):
    return -(-value // step) * step


def exchange_kernel(
    n_lat,
    n_fld,
    lane_tile,
    sizes,
    x_ref,
    points_ref,
    waves_ref,
    owned_ref,
    legendre_ref,
    out_ref,
    *scratch,
):
    n_groups = len(sizes)
    send_bufs, scratch = scratch[:n_groups], scratch[n_groups:]
    recv_bufs, scratch = scratch[:n_groups], scratch[n_groups:]
    (
        wave_cols,
        tables,
        mixed_sym,
        mixed_anti,
        rows_sym,
        rows_anti,
        partial,
        part_send,
        part_recv,
        send_sem,
        recv_sem,
        table_sem,
        part_send_sem,
        part_recv_sem,
    ) = scratch
    lat = lax.axis_index("lat")
    fld = lax.axis_index("fld")
    half = n_lat // 2
    depth = half // n_fld
    sources = 2 * depth
    hemi = lat // half
    block = (lat % half) // depth
    place = lat % depth
    columns, wave_count = x_ref.shape
    owner_waves = sum(sizes)
    kinds = part_send.shape[1]
    rows_each = columns // kinds
    pairs = owner_waves // 2
    own = block == fld
    lat_depth, total = legendre_ref.shape
    first_owned = lat * owner_waves

    load = pltpu.make_async_copy(legendre_ref, tables, table_sem)
    load.start()

    barrier = pltpu.get_barrier_semaphore()

    def greet(s, carry):
        source_fld = s // sources
        rest = s % sources
        source_lat = (rest // depth) * half + fld * depth + rest % depth
        itself = jnp.logical_and(source_lat == lat, source_fld == fld)

        @pl.when(jnp.logical_not(itself))
        def _():
            pl.semaphore_signal(
                barrier, inc=1, device_id=(source_lat, source_fld), device_id_type=MESH
            )

        return carry

    lax.fori_loop(0, n_fld * sources, greet, 0)
    for d in range(1, n_fld):
        pl.semaphore_signal(
            barrier, inc=1, device_id=(lat, (fld + d) % n_fld), device_id_type=MESH
        )

    slot = fld * sources + hemi * depth + place

    def copy_to(number, owner):
        return pltpu.make_async_remote_copy(
            src_ref=send_bufs[number].at[owner],
            dst_ref=recv_bufs[number].at[slot],
            send_sem=send_sem.at[number, owner],
            recv_sem=recv_sem.at[number, slot],
            device_id=(owner, block),
            device_id_type=MESH,
        )

    for v in range(-(-wave_count // 128)):
        width = min(128, wave_count - 128 * v)
        line = waves_ref[128 * v : 128 * v + width].reshape(1, width)
        wave_cols[128 * v : 128 * v + width] = jnp.broadcast_to(line, (128, width)).T

    wave_cols[wave_count : wave_count + 8] = jnp.full((8, 128), -1, jnp.int32)

    lane = lax.broadcasted_iota(jnp.int32, (n_lat * 8, 128), 1)
    points = points_ref[...].reshape(1, rows_each)
    limit = jnp.minimum(lax.shift_right_logical(points, 1), wave_count)
    limit = jnp.concatenate([limit] * kinds, axis=1)

    def reorder(number):
        first = 8 * number
        wave = jnp.concatenate(
            [wave_cols[o * owner_waves + first : o * owner_waves + first + 8] for o in range(n_lat)],
            axis=0,
        )
        pieces = []
        for v in range(-(-wave_count // 128)):
            width = min(128, wave_count - 128 * v)
            hit = jnp.where(wave == lane + 128 * v, 1.0, 0.0).astype(jnp.bfloat16)
            pieces.append(hit[:, :width])
        chosen = jnp.concatenate(pieces, axis=1)
        picked = lax.dot_general(
            chosen, x_ref[...], NT, preferred_element_type=jnp.float32
        )
        wide = jnp.concatenate([wave] * (-(-columns // 128)), axis=1)[:, :columns]
        picked = jnp.where(wide < limit, picked, 0.0)
        for o in range(n_lat):
            part = picked[8 * o : 8 * o + sizes[number]]
            send_bufs[number][o] = part.astype(jnp.bfloat16)

    def send(number):
        def several(u, carry):
            for n in range(8):
                if n_lat == 64:
                    owner = (
                        (lat // 16 + u % 4 + n) % 4 * 16
                        + (lat // 2 % 8 + (4, 1, 7, 2, 6, 3, 5, 0)[n]) % 8 * 2
                        + (lat + u // 4 + n) % 2
                    )
                else:
                    owner = (lat + u * 8 + n) % n_lat
                itself = jnp.logical_and(own, owner == lat)

                @pl.when(itself)
                def _():
                    pltpu.make_async_copy(
                        send_bufs[number].at[owner],
                        recv_bufs[number].at[slot],
                        recv_sem.at[number, slot],
                    ).start()

                @pl.when(jnp.logical_not(itself))
                def _():
                    copy_to(number, owner).start()

            return carry

        lax.fori_loop(0, n_lat // 8, several, 0)

    for number in range(n_groups):
        reorder(number)
        if number == 0:
            pl.semaphore_wait(barrier, n_lat + n_fld - 1 - own.astype(jnp.int32))
        send(number)

    def gather_group(number):
        count = sizes[number]
        recv_buf = recv_bufs[number]

        def gather_field(f, carry):
            def arrived(s, carry):
                at = f * sources + s
                pltpu.make_async_copy(
                    recv_buf.at[at], recv_buf.at[at], recv_sem.at[number, at]
                ).wait()
                return carry

            lax.fori_loop(0, sources, arrived, 0)
            for a in range(depth):
                north = recv_buf[f * sources + a].astype(jnp.float32)
                south = recv_buf[f * sources + depth + a].astype(jnp.float32)
                mixed_sym[a, 0:count] = north + south
                mixed_anti[a, 0:count] = north - south
            for mixed, rows in ((mixed_sym, rows_sym), (mixed_anti, rows_anti)):
                for k in range(kinds):
                    lo = k * rows_each
                    joined = jnp.concatenate(
                        [mixed[a, 0:count, lo : lo + rows_each] for a in range(depth)], axis=1
                    )
                    start = 8 * number * n_fld * kinds + f * kinds + k
                    for v in range(-(-lat_depth // 128)):
                        width = min(128, lat_depth - 128 * v)
                        rows[v, pl.ds(start, count, stride=n_fld * kinds), 0:width] = joined[
                            :, 128 * v : 128 * v + width
                        ]
            return carry

        lax.fori_loop(0, n_fld, gather_field, 0)

    per_wave = n_fld * kinds
    even = wave_count // 2 + 1
    sym_end = round_up(even + pairs, lane_tile)
    anti_start = even // lane_tile * lane_tile

    def operand(rows, pair):
        start = pl.multiple_of(pair * (2 * per_wave), 2 * per_wave)
        parts = []
        for v in range(-(-lat_depth // 128)):
            width = min(128, lat_depth - 128 * v)
            parts.append(rows[v, pl.ds(start, 2 * per_wave), 0:width])
        return jnp.concatenate(parts, axis=1).astype(jnp.bfloat16)

    def project(left, start, width):
        return jnp.dot(left, tables[:, pl.ds(start, width)], preferred_element_type=jnp.float32)

    def choose(product, first):
        return jnp.where(first, product[:per_wave], product[per_wave:])

    def degree_index(width, offset):
        return lax.broadcasted_iota(jnp.int32, (per_wave, width), 1) + offset

    def part_copy(d, lo, width, number):
        peer = (fld + d) % n_fld
        return pltpu.make_async_remote_copy(
            src_ref=part_send.at[peer, :, pl.ds(lo, width)],
            dst_ref=part_recv.at[d - 1, :, pl.ds(lo, width)],
            send_sem=part_send_sem.at[d - 1, number],
            recv_sem=part_recv_sem.at[d - 1, number],
            device_id=(lat, peer),
            device_id_type=MESH,
        )

    def left_over(pair, start, width):
        first_rows = lax.shift_right_logical(wave_count - owned_ref[first_owned + 2 * pair], 1)
        product = project(operand(rows_anti, pair), start, width)
        degree = degree_index(width, 0) + (wave_count // 2 - 1 - pair)
        return choose(product, degree < first_rows)

    def pair_chunk(c, carry):
        start = pl.multiple_of(c * wave_count, min(wave_count, 1280))
        wave = owned_ref[first_owned + 2 * c]
        first_even = lax.shift_right_logical(wave_count + 1 - wave, 1)
        first_odd = lax.shift_right_logical(wave_count - wave, 1)
        sym = project(operand(rows_sym, c), start, sym_end)
        sym = choose(sym, degree_index(sym_end, -c) < first_even)
        anti_width = wave_count - anti_start
        anti_from = pl.multiple_of(start + anti_start, lane_tile)
        anti = project(operand(rows_anti, c), anti_from, anti_width)
        anti = choose(anti, degree_index(anti_width, anti_start - even - c) < first_odd)
        before = left_over(jnp.maximum(c - 1, 0), start, lane_tile)
        head = jnp.where(degree_index(lane_tile, 0) < c, before, sym[:, :lane_tile])
        middle = jnp.where(
            degree_index(sym_end - anti_start, anti_start - c) < even,
            sym[:, anti_start:],
            anti[:, : sym_end - anti_start],
        )
        pieces = [head, sym[:, lane_tile:anti_start], middle, anti[:, sym_end - anti_start :]]
        at = 0
        for piece in pieces:
            width = piece.shape[1]
            if width == 0:
                continue
            lanes = pl.ds(pl.multiple_of(start + at, lane_tile), width)
            partial[:, lanes] = piece
            for f in range(n_fld):
                part_send[f, :, lanes] = piece[f * kinds : (f + 1) * kinds].astype(jnp.bfloat16)
            at += width
        for d in range(1, n_fld):
            part_copy(d, start, wave_count, c).start()
        return carry

    tail = total - pairs * wave_count
    tail_from = pairs * wave_count
    tail_wide = part_send.shape[2] - tail_from

    mine = pl.multiple_of(fld * kinds, kinds)
    batch_rows = kinds // 2

    def finish(lo, width, kept, number):
        for d in range(1, n_fld):
            part_copy(d, lo, width, number).wait_recv()
        result = partial[pl.ds(mine, kinds), pl.ds(lo, kept)]
        for d in range(1, n_fld):
            result = result + part_recv[d - 1, :, pl.ds(lo, kept)].astype(jnp.float32)
        out_ref[0, :, pl.ds(lo, kept)] = result[:batch_rows]
        out_ref[1, :, pl.ds(lo, kept)] = result[batch_rows:]

    def finish_pair(c, carry):
        start = pl.multiple_of(c * wave_count, min(wave_count, 1280))
        finish(start, wave_count, wave_count, c)
        return carry

    load.wait()
    finished = 0
    for number in range(n_groups):
        gather_group(number)
        first = 4 * number
        lax.fori_loop(first, first + sizes[number] // 2, pair_chunk, 0)
        if number == n_groups - 2:
            finished = 4 * number
            lax.fori_loop(0, finished, finish_pair, 0)

    piece = left_over(pairs - 1, tail_from, tail)
    partial[:, tail_from : tail_from + tail] = piece
    for f in range(n_fld):
        part_send[f, :, tail_from : tail_from + tail] = piece[
            f * kinds : (f + 1) * kinds
        ].astype(jnp.bfloat16)
    for d in range(1, n_fld):
        part_copy(d, tail_from, tail_wide, pairs).start()

    lax.fori_loop(finished, pairs, finish_pair, 0)
    finish(tail_from, tail_wide, tail, pairs)

    for number in range(n_groups):

        def sent(owner, carry):
            @pl.when(jnp.logical_not(jnp.logical_and(own, owner == lat)))
            def _():
                copy_to(number, owner).wait_send()

            return carry

        lax.fori_loop(0, n_lat, sent, 0)

    def part_sent(c, carry):
        start = pl.multiple_of(c * wave_count, min(wave_count, 1280))
        for d in range(1, n_fld):
            part_copy(d, start, wave_count, c).wait_send()
        return carry

    lax.fori_loop(0, pairs, part_sent, 0)
    for d in range(1, n_fld):
        part_copy(d, tail_from, tail_wide, pairs).wait_send()


def shards(fourier, legendre, cycle_points, wave_order, lane_tile=256):
    n_lat, n_fld = lax.axis_size("lat"), lax.axis_size("fld")
    batches, rows_each, fields, parts, wave_count = fourier.shape
    kinds = batches * fields * parts
    columns = kinds * rows_each
    owner_waves = wave_count // n_lat
    total, lat_depth = legendre.shape
    depth = n_lat // 2 // n_fld
    slots = 2 * depth * n_fld
    per_wave = n_fld * kinds
    padded = round_up(total, 128)
    tiles = -(-lat_depth // 128)

    sizes = tuple(min(8, owner_waves - t) for t in range(0, owner_waves, 8))
    x = jnp.transpose(fourier, (0, 2, 3, 1, 4)).reshape(columns, wave_count)
    vmem = pl.BlockSpec(memory_space=pltpu.VMEM)
    return pl.pallas_call(
        functools.partial(exchange_kernel, n_lat, n_fld, lane_tile, sizes),
        out_shape=jax.ShapeDtypeStruct((batches, fields * parts, total), jnp.float32),
        in_specs=[
            vmem,
            vmem,
            vmem,
            pl.BlockSpec(memory_space=pltpu.SMEM),
            pl.BlockSpec(memory_space=pltpu.HBM),
        ],
        out_specs=vmem,
        scratch_shapes=[
            *(pltpu.VMEM((n_lat, count, columns), jnp.bfloat16) for count in sizes),
            *(pltpu.VMEM((slots, count, columns), jnp.bfloat16) for count in sizes),
            pltpu.VMEM((round_up(wave_count, 128) + 8, 128), jnp.int32),
            pltpu.VMEM((lat_depth, total), jnp.bfloat16),
            pltpu.VMEM((depth, 8, columns), jnp.float32),
            pltpu.VMEM((depth, 8, columns), jnp.float32),
            pltpu.VMEM((tiles, owner_waves * per_wave, 128), jnp.float32),
            pltpu.VMEM((tiles, owner_waves * per_wave, 128), jnp.float32),
            pltpu.VMEM((per_wave, padded), jnp.float32),
            pltpu.VMEM((n_fld, kinds, padded), jnp.bfloat16),
            pltpu.VMEM((n_fld - 1, kinds, padded), jnp.bfloat16),
            pltpu.SemaphoreType.DMA((len(sizes), n_lat)),
            pltpu.SemaphoreType.DMA((len(sizes), slots)),
            pltpu.SemaphoreType.DMA,
            pltpu.SemaphoreType.DMA((n_fld - 1, owner_waves // 2 + 1)),
            pltpu.SemaphoreType.DMA((n_fld - 1, owner_waves // 2 + 1)),
        ],
        compiler_params=pltpu.CompilerParams(
            collective_id=0, has_side_effects=True, vmem_limit_bytes=48 * 2**20
        ),
        cost_estimate=pl.CostEstimate(
            flops=4 * columns * wave_count * wave_count,
            bytes_accessed=total * lat_depth * 2,
            transcendentals=0,
        ),
    )(x, cycle_points, wave_order, wave_order, legendre.T)


def solution(mesh):
    placed = (P(None, "lat", "fld", None, None), P("lat", "fld"), P("lat"), P())
    return jax.shard_map(
        shards, mesh=mesh, in_specs=placed, out_specs=P(None, "fld", "lat"), check_vma=False
    )
```

```python
import functools

import jax
import jax.numpy as jnp
from jax import lax
from jax.experimental import pallas as pl
from jax.experimental.pallas import tpu as pltpu
from jax.sharding import PartitionSpec as P

MESH = pl.DeviceIdType.MESH
NT = (((1,), (1,)), ((), ()))


def round_up(value, step):
    return -(-value // step) * step


def exchange_kernel(
    n_lat,
    n_fld,
    lane_tile,
    sizes,
    x_ref,
    points_ref,
    waves_ref,
    owned_ref,
    legendre_ref,
    out_ref,
    *scratch,
):
    n_groups = len(sizes)
    send_bufs, scratch = scratch[:n_groups], scratch[n_groups:]
    recv_bufs, scratch = scratch[:n_groups], scratch[n_groups:]
    (
        wave_cols,
        tables,
        mixed_sym,
        mixed_anti,
        rows_sym,
        rows_anti,
        partial,
        part_send,
        part_recv,
        send_sem,
        recv_sem,
        table_sem,
        part_send_sem,
        part_recv_sem,
    ) = scratch
    lat = lax.axis_index("lat")
    fld = lax.axis_index("fld")
    half = n_lat // 2
    depth = half // n_fld
    sources = 2 * depth
    hemi = lat // half
    block = (lat % half) // depth
    place = lat % depth
    columns, wave_count = x_ref.shape
    owner_waves = sum(sizes)
    kinds = part_send.shape[1]
    rows_each = columns // kinds
    pairs = owner_waves // 2
    own = block == fld
    lat_depth, total = legendre_ref.shape
    first_owned = lat * owner_waves

    load = pltpu.make_async_copy(legendre_ref, tables, table_sem)
    load.start()

    barrier = pltpu.get_barrier_semaphore()

    def greet(s, carry):
        source_fld = s // sources
        rest = s % sources
        source_lat = (rest // depth) * half + fld * depth + rest % depth
        itself = jnp.logical_and(source_lat == lat, source_fld == fld)

        @pl.when(jnp.logical_not(itself))
        def _():
            pl.semaphore_signal(
                barrier, inc=1, device_id=(source_lat, source_fld), device_id_type=MESH
            )

        return carry

    lax.fori_loop(0, n_fld * sources, greet, 0)
    for d in range(1, n_fld):
        pl.semaphore_signal(
            barrier, inc=1, device_id=(lat, (fld + d) % n_fld), device_id_type=MESH
        )

    slot = fld * sources + hemi * depth + place

    def copy_to(number, batch, owner):
        return pltpu.make_async_remote_copy(
            src_ref=send_bufs[number].at[owner],
            dst_ref=recv_bufs[number].at[slot],
            send_sem=send_sem.at[number, batch],
            recv_sem=recv_sem.at[number, fld],
            device_id=(owner, block),
            device_id_type=MESH,
        )

    for v in range(-(-wave_count // 128)):
        width = min(128, wave_count - 128 * v)
        line = waves_ref[128 * v : 128 * v + width].reshape(1, width)
        wave_cols[128 * v : 128 * v + width] = jnp.broadcast_to(line, (128, width)).T

    wave_cols[wave_count : wave_count + 8] = jnp.full((8, 128), -1, jnp.int32)

    lane = lax.broadcasted_iota(jnp.int32, (n_lat * 8, 128), 1)
    points = points_ref[...].reshape(1, rows_each)
    limit = jnp.minimum(lax.shift_right_logical(points, 1), wave_count)
    limit = jnp.concatenate([limit] * kinds, axis=1)

    def reorder(number):
        first = 8 * number
        wave = jnp.concatenate(
            [wave_cols[o * owner_waves + first : o * owner_waves + first + 8] for o in range(n_lat)],
            axis=0,
        )
        pieces = []
        for v in range(-(-wave_count // 128)):
            width = min(128, wave_count - 128 * v)
            hit = jnp.where(wave == lane + 128 * v, 1.0, 0.0).astype(jnp.bfloat16)
            pieces.append(hit[:, :width])
        chosen = jnp.concatenate(pieces, axis=1)
        picked = lax.dot_general(
            chosen, x_ref[...], NT, preferred_element_type=jnp.float32
        )
        wide = jnp.concatenate([wave] * (-(-columns // 128)), axis=1)[:, :columns]
        picked = jnp.where(wide < limit, picked, 0.0)
        for o in range(n_lat):
            part = picked[8 * o : 8 * o + sizes[number]]
            send_bufs[number][o] = part.astype(jnp.bfloat16)

    batches = n_lat // 8
    own_batch, own_step = (5, 7) if n_lat == 64 else (0, 0)

    def target(batch, n):
        if n_lat != 64:
            return (lat + batch * 8 + n) % n_lat
        x = (lat // 16 + batch % 4 + n) % 4
        z = (lat // 2 % 8 + (4, 1, 7, 2, 6, 3, 5, 0)[n]) % 8
        return x * 16 + z * 2 + (lat + batch // 4 + n) % 2

    def left(number, batch):
        buf = send_bufs[number]
        less = jnp.logical_and(own, batch == own_batch)

        @pl.when(less)
        def _():
            done = buf.at[pl.ds(0, 7)]
            pltpu.make_async_copy(done, done, send_sem.at[number, batch]).wait()

        @pl.when(jnp.logical_not(less))
        def _():
            done = buf.at[pl.ds(0, 8)]
            pltpu.make_async_copy(done, done, send_sem.at[number, batch]).wait()

    def send(number, after=None):
        def several(batch, carry):
            if after is not None:
                left(after, batch)
            for n in range(8):
                owner = target(batch, n)
                if n != own_step:
                    copy_to(number, batch, owner).start()
                    continue
                itself = jnp.logical_and(own, batch == own_batch)

                @pl.when(itself)
                def _():
                    pltpu.make_async_copy(
                        send_bufs[number].at[owner],
                        recv_bufs[number].at[slot],
                        recv_sem.at[number, fld],
                    ).start()

                @pl.when(jnp.logical_not(itself))
                def _():
                    copy_to(number, batch, owner).start()

            return carry

        lax.fori_loop(0, batches, several, 0)

    for number in range(n_groups):
        reorder(number)
        if number == 0:
            pl.semaphore_wait(barrier, n_lat + n_fld - 1 - own.astype(jnp.int32))
            send(number)
    send(1, 0)

    def gather_group(number):
        count = sizes[number]
        recv_buf = recv_bufs[number]

        def gather_field(f, carry):
            here = recv_buf.at[pl.ds(f * sources, sources)]
            pltpu.make_async_copy(here, here, recv_sem.at[number, f]).wait()
            for a in range(depth):
                north = recv_buf[f * sources + a].astype(jnp.float32)
                south = recv_buf[f * sources + depth + a].astype(jnp.float32)
                mixed_sym[a, 0:count] = north + south
                mixed_anti[a, 0:count] = north - south
            for mixed, rows in ((mixed_sym, rows_sym), (mixed_anti, rows_anti)):
                for k in range(kinds):
                    lo = k * rows_each
                    joined = jnp.concatenate(
                        [mixed[a, 0:count, lo : lo + rows_each] for a in range(depth)], axis=1
                    )
                    start = 8 * number * n_fld * kinds + f * kinds + k
                    for v in range(-(-lat_depth // 128)):
                        width = min(128, lat_depth - 128 * v)
                        rows[v, pl.ds(start, count, stride=n_fld * kinds), 0:width] = joined[
                            :, 128 * v : 128 * v + width
                        ]
            return carry

        lax.fori_loop(0, n_fld, gather_field, 0)

    per_wave = n_fld * kinds
    even = wave_count // 2 + 1
    sym_end = round_up(even + pairs, lane_tile)
    anti_start = even // lane_tile * lane_tile

    def operand(rows, pair):
        start = pl.multiple_of(pair * (2 * per_wave), 2 * per_wave)
        parts = []
        for v in range(-(-lat_depth // 128)):
            width = min(128, lat_depth - 128 * v)
            parts.append(rows[v, pl.ds(start, 2 * per_wave), 0:width])
        return jnp.concatenate(parts, axis=1).astype(jnp.bfloat16)

    def project(left, start, width):
        return jnp.dot(left, tables[:, pl.ds(start, width)], preferred_element_type=jnp.float32)

    def choose(product, first):
        return jnp.where(first, product[:per_wave], product[per_wave:])

    def degree_index(width, offset):
        return lax.broadcasted_iota(jnp.int32, (per_wave, width), 1) + offset

    def part_copy(d, lo, width, number):
        peer = (fld + d) % n_fld
        return pltpu.make_async_remote_copy(
            src_ref=part_send.at[peer, :, pl.ds(lo, width)],
            dst_ref=part_recv.at[d - 1, :, pl.ds(lo, width)],
            send_sem=part_send_sem.at[d - 1],
            recv_sem=part_recv_sem.at[d - 1, number],
            device_id=(lat, peer),
            device_id_type=MESH,
        )

    def left_over(pair, start, width):
        first_rows = lax.shift_right_logical(wave_count - owned_ref[first_owned + 2 * pair], 1)
        product = project(operand(rows_anti, pair), start, width)
        degree = degree_index(width, 0) + (wave_count // 2 - 1 - pair)
        return choose(product, degree < first_rows)

    def pair_chunk(c, carry):
        start = pl.multiple_of(c * wave_count, min(wave_count, 1280))
        wave = owned_ref[first_owned + 2 * c]
        first_even = lax.shift_right_logical(wave_count + 1 - wave, 1)
        first_odd = lax.shift_right_logical(wave_count - wave, 1)
        sym = project(operand(rows_sym, c), start, sym_end)
        sym = choose(sym, degree_index(sym_end, -c) < first_even)
        anti_width = wave_count - anti_start
        anti_from = pl.multiple_of(start + anti_start, lane_tile)
        anti = project(operand(rows_anti, c), anti_from, anti_width)
        anti = choose(anti, degree_index(anti_width, anti_start - even - c) < first_odd)
        before = left_over(jnp.maximum(c - 1, 0), start, lane_tile)
        head = jnp.where(degree_index(lane_tile, 0) < c, before, sym[:, :lane_tile])
        middle = jnp.where(
            degree_index(sym_end - anti_start, anti_start - c) < even,
            sym[:, anti_start:],
            anti[:, : sym_end - anti_start],
        )
        pieces = [head, sym[:, lane_tile:anti_start], middle, anti[:, sym_end - anti_start :]]
        at = 0
        for piece in pieces:
            width = piece.shape[1]
            if width == 0:
                continue
            lanes = pl.ds(pl.multiple_of(start + at, lane_tile), width)
            partial[:, lanes] = piece
            for f in range(n_fld):
                part_send[f, :, lanes] = piece[f * kinds : (f + 1) * kinds].astype(jnp.bfloat16)
            at += width
        for d in range(1, n_fld):
            part_copy(d, start, wave_count, c).start()
        return carry

    tail = total - pairs * wave_count
    tail_from = pairs * wave_count
    tail_wide = part_send.shape[2] - tail_from

    mine = pl.multiple_of(fld * kinds, kinds)
    batch_rows = kinds // 2

    def finish(lo, width, kept, number):
        for d in range(1, n_fld):
            part_copy(d, lo, width, number).wait_recv()
        result = partial[pl.ds(mine, kinds), pl.ds(lo, kept)]
        for d in range(1, n_fld):
            result = result + part_recv[d - 1, :, pl.ds(lo, kept)].astype(jnp.float32)
        out_ref[0, :, pl.ds(lo, kept)] = result[:batch_rows]
        out_ref[1, :, pl.ds(lo, kept)] = result[batch_rows:]

    def finish_pair(c, carry):
        start = pl.multiple_of(c * wave_count, min(wave_count, 1280))
        finish(start, wave_count, wave_count, c)
        return carry

    load.wait()
    finished = 0
    for number in range(n_groups):
        gather_group(number)
        first = 4 * number
        lax.fori_loop(first, first + sizes[number] // 2, pair_chunk, 0)
        if number + 2 < n_groups:
            send(number + 2, number + 1)
        if number == n_groups - 2:
            finished = 4 * number
            lax.fori_loop(0, finished, finish_pair, 0)

    piece = left_over(pairs - 1, tail_from, tail)
    partial[:, tail_from : tail_from + tail] = piece
    for f in range(n_fld):
        part_send[f, :, tail_from : tail_from + tail] = piece[
            f * kinds : (f + 1) * kinds
        ].astype(jnp.bfloat16)
    for d in range(1, n_fld):
        part_copy(d, tail_from, tail_wide, pairs).start()

    def last_left(batch, carry):
        left(n_groups - 1, batch)
        return carry

    lax.fori_loop(0, batches, last_left, 0)
    lax.fori_loop(finished, pairs, finish_pair, 0)
    finish(tail_from, tail_wide, tail, pairs)
    for d in range(1, n_fld):
        whole = part_send.at[(fld + d) % n_fld]
        pltpu.make_async_copy(whole, whole, part_send_sem.at[d - 1]).wait()


def shards(fourier, legendre, cycle_points, wave_order, lane_tile=256):
    n_lat, n_fld = lax.axis_size("lat"), lax.axis_size("fld")
    batches, rows_each, fields, parts, wave_count = fourier.shape
    kinds = batches * fields * parts
    columns = kinds * rows_each
    owner_waves = wave_count // n_lat
    total, lat_depth = legendre.shape
    depth = n_lat // 2 // n_fld
    slots = 2 * depth * n_fld
    per_wave = n_fld * kinds
    padded = round_up(total, 128)
    tiles = -(-lat_depth // 128)

    sizes = tuple(min(8, owner_waves - t) for t in range(0, owner_waves, 8))
    x = jnp.transpose(fourier, (0, 2, 3, 1, 4)).reshape(columns, wave_count)
    vmem = pl.BlockSpec(memory_space=pltpu.VMEM)
    return pl.pallas_call(
        functools.partial(exchange_kernel, n_lat, n_fld, lane_tile, sizes),
        out_shape=jax.ShapeDtypeStruct((batches, fields * parts, total), jnp.float32),
        in_specs=[
            vmem,
            vmem,
            vmem,
            pl.BlockSpec(memory_space=pltpu.SMEM),
            pl.BlockSpec(memory_space=pltpu.HBM),
        ],
        out_specs=vmem,
        scratch_shapes=[
            *(pltpu.VMEM((n_lat, count, columns), jnp.bfloat16) for count in sizes),
            *(pltpu.VMEM((slots, count, columns), jnp.bfloat16) for count in sizes),
            pltpu.VMEM((round_up(wave_count, 128) + 8, 128), jnp.int32),
            pltpu.VMEM((lat_depth, total), jnp.bfloat16),
            pltpu.VMEM((depth, 8, columns), jnp.float32),
            pltpu.VMEM((depth, 8, columns), jnp.float32),
            pltpu.VMEM((tiles, owner_waves * per_wave, 128), jnp.float32),
            pltpu.VMEM((tiles, owner_waves * per_wave, 128), jnp.float32),
            pltpu.VMEM((per_wave, padded), jnp.float32),
            pltpu.VMEM((n_fld, kinds, padded), jnp.bfloat16),
            pltpu.VMEM((n_fld - 1, kinds, padded), jnp.bfloat16),
            pltpu.SemaphoreType.DMA((len(sizes), n_lat // 8)),
            pltpu.SemaphoreType.DMA((len(sizes), n_fld)),
            pltpu.SemaphoreType.DMA,
            pltpu.SemaphoreType.DMA((n_fld - 1,)),
            pltpu.SemaphoreType.DMA((n_fld - 1, owner_waves // 2 + 1)),
        ],
        compiler_params=pltpu.CompilerParams(
            collective_id=0, has_side_effects=True, vmem_limit_bytes=48 * 2**20
        ),
        cost_estimate=pl.CostEstimate(
            flops=4 * columns * wave_count * wave_count,
            bytes_accessed=total * lat_depth * 2,
            transcendentals=0,
        ),
    )(x, cycle_points, wave_order, wave_order, legendre.T)


def solution(mesh):
    placed = (P(None, "lat", "fld", None, None), P("lat", "fld"), P("lat"), P())
    return jax.shard_map(
        shards, mesh=mesh, in_specs=placed, out_specs=P(None, "fld", "lat"), check_vma=False
    )
```

```python
import functools

import jax
import jax.numpy as jnp
from jax import lax
from jax.experimental import pallas as pl
from jax.experimental.pallas import tpu as pltpu
from jax.sharding import PartitionSpec as P

MESH = pl.DeviceIdType.MESH
NT = (((1,), (1,)), ((), ()))
GROUPS = (4, 4, 4, 4, 4)


def round_up(value, step):
    return -(-value // step) * step


def exchange_kernel(
    n_lat,
    n_fld,
    lane_tile,
    sizes,
    x_ref,
    points_ref,
    waves_ref,
    owned_ref,
    legendre_ref,
    out_ref,
    *scratch,
):
    n_groups = len(sizes)
    send_bufs, scratch = scratch[:n_groups], scratch[n_groups:]
    recv_bufs, scratch = scratch[:n_groups], scratch[n_groups:]
    (
        wave_cols,
        tables,
        mixed_sym,
        mixed_anti,
        rows_sym,
        rows_anti,
        partial,
        part_send,
        part_recv,
        send_sem,
        recv_sem,
        table_sem,
        part_send_sem,
        part_recv_sem,
    ) = scratch
    lat = lax.axis_index("lat")
    fld = lax.axis_index("fld")
    half = n_lat // 2
    depth = half // n_fld
    sources = 2 * depth
    hemi = lat // half
    block = (lat % half) // depth
    place = lat % depth
    columns, wave_count = x_ref.shape
    owner_waves = sum(sizes)
    firsts = [sum(sizes[:number]) for number in range(n_groups)]
    kinds = part_send.shape[1]
    rows_each = columns // kinds
    pairs = owner_waves // 2
    own = block == fld
    lat_depth, total = legendre_ref.shape
    first_owned = lat * owner_waves

    load = pltpu.make_async_copy(legendre_ref, tables, table_sem)
    load.start()

    barrier = pltpu.get_barrier_semaphore()

    def greet(s, carry):
        source_fld = s // sources
        rest = s % sources
        source_lat = (rest // depth) * half + fld * depth + rest % depth
        itself = jnp.logical_and(source_lat == lat, source_fld == fld)

        @pl.when(jnp.logical_not(itself))
        def _():
            pl.semaphore_signal(
                barrier, inc=1, device_id=(source_lat, source_fld), device_id_type=MESH
            )

        return carry

    lax.fori_loop(0, n_fld * sources, greet, 0)
    for d in range(1, n_fld):
        pl.semaphore_signal(
            barrier, inc=1, device_id=(lat, (fld + d) % n_fld), device_id_type=MESH
        )

    slot = fld * sources + hemi * depth + place

    def copy_to(number, batch, owner):
        return pltpu.make_async_remote_copy(
            src_ref=send_bufs[number].at[owner],
            dst_ref=recv_bufs[number].at[slot],
            send_sem=send_sem.at[number, batch],
            recv_sem=recv_sem.at[number, fld],
            device_id=(owner, block),
            device_id_type=MESH,
        )

    for v in range(-(-wave_count // 128)):
        width = min(128, wave_count - 128 * v)
        line = waves_ref[128 * v : 128 * v + width].reshape(1, width)
        wave_cols[128 * v : 128 * v + width] = jnp.broadcast_to(line, (128, width)).T

    wave_cols[wave_count : wave_count + 8] = jnp.full((8, 128), -1, jnp.int32)

    lane = lax.broadcasted_iota(jnp.int32, (n_lat * 8, 128), 1)
    points = points_ref[...].reshape(1, rows_each)
    limit = jnp.minimum(lax.shift_right_logical(points, 1), wave_count)
    limit = jnp.concatenate([limit] * kinds, axis=1)

    def reorder(number):
        first = firsts[number]
        wave = jnp.concatenate(
            [wave_cols[o * owner_waves + first : o * owner_waves + first + 8] for o in range(n_lat)],
            axis=0,
        )
        pieces = []
        for v in range(-(-wave_count // 128)):
            width = min(128, wave_count - 128 * v)
            hit = jnp.where(wave == lane + 128 * v, 1.0, 0.0).astype(jnp.bfloat16)
            pieces.append(hit[:, :width])
        chosen = jnp.concatenate(pieces, axis=1)
        picked = lax.dot_general(
            chosen, x_ref[...], NT, preferred_element_type=jnp.float32
        )
        wide = jnp.concatenate([wave] * (-(-columns // 128)), axis=1)[:, :columns]
        picked = jnp.where(wide < limit, picked, 0.0)
        for o in range(n_lat):
            part = picked[8 * o : 8 * o + sizes[number]]
            send_bufs[number][o] = part.astype(jnp.bfloat16)

    batches = n_lat // 8
    own_batch, own_step = (5, 7) if n_lat == 64 else (0, 0)

    def target(batch, n):
        if n_lat != 64:
            return (lat + batch * 8 + n) % n_lat
        x = (lat // 16 + batch % 4 + n) % 4
        z = (lat // 2 % 8 + (4, 1, 7, 2, 6, 3, 5, 0)[n]) % 8
        return x * 16 + z * 2 + (lat + batch // 4 + n) % 2

    def left(number, batch):
        buf = send_bufs[number]
        less = jnp.logical_and(own, batch == own_batch)

        @pl.when(less)
        def _():
            done = buf.at[pl.ds(0, 7)]
            pltpu.make_async_copy(done, done, send_sem.at[number, batch]).wait()

        @pl.when(jnp.logical_not(less))
        def _():
            done = buf.at[pl.ds(0, 8)]
            pltpu.make_async_copy(done, done, send_sem.at[number, batch]).wait()

    def send(number, after=None):
        def several(batch, carry):
            if after is not None:
                left(after, batch)
            for n in range(8):
                owner = target(batch, n)
                if n != own_step:
                    copy_to(number, batch, owner).start()
                    continue
                itself = jnp.logical_and(own, batch == own_batch)

                @pl.when(itself)
                def _():
                    pltpu.make_async_copy(
                        send_bufs[number].at[owner],
                        recv_bufs[number].at[slot],
                        recv_sem.at[number, fld],
                    ).start()

                @pl.when(jnp.logical_not(itself))
                def _():
                    copy_to(number, batch, owner).start()

            return carry

        lax.fori_loop(0, batches, several, 0)

    for number in range(n_groups):
        reorder(number)
        if number == 0:
            pl.semaphore_wait(barrier, n_lat + n_fld - 1 - own.astype(jnp.int32))
            send(number)
    send(1, 0)

    def gather_group(number):
        count = sizes[number]
        recv_buf = recv_bufs[number]

        def gather_field(f, carry):
            here = recv_buf.at[pl.ds(f * sources, sources)]
            pltpu.make_async_copy(here, here, recv_sem.at[number, f]).wait()
            for a in range(depth):
                north = recv_buf[f * sources + a].astype(jnp.float32)
                south = recv_buf[f * sources + depth + a].astype(jnp.float32)
                mixed_sym[a, 0:count] = north + south
                mixed_anti[a, 0:count] = north - south
            for mixed, rows in ((mixed_sym, rows_sym), (mixed_anti, rows_anti)):
                for k in range(kinds):
                    lo = k * rows_each
                    joined = jnp.concatenate(
                        [mixed[a, 0:count, lo : lo + rows_each] for a in range(depth)], axis=1
                    )
                    start = firsts[number] * n_fld * kinds + f * kinds + k
                    for v in range(-(-lat_depth // 128)):
                        width = min(128, lat_depth - 128 * v)
                        rows[v, pl.ds(start, count, stride=n_fld * kinds), 0:width] = joined[
                            :, 128 * v : 128 * v + width
                        ]
            return carry

        lax.fori_loop(0, n_fld, gather_field, 0)

    per_wave = n_fld * kinds
    even = wave_count // 2 + 1
    sym_end = round_up(even + pairs, lane_tile)
    anti_start = even // lane_tile * lane_tile

    def operand(rows, pair):
        start = pl.multiple_of(pair * (2 * per_wave), 2 * per_wave)
        parts = []
        for v in range(-(-lat_depth // 128)):
            width = min(128, lat_depth - 128 * v)
            parts.append(rows[v, pl.ds(start, 2 * per_wave), 0:width])
        return jnp.concatenate(parts, axis=1).astype(jnp.bfloat16)

    def project(left, start, width):
        return jnp.dot(left, tables[:, pl.ds(start, width)], preferred_element_type=jnp.float32)

    def choose(product, first):
        return jnp.where(first, product[:per_wave], product[per_wave:])

    def degree_index(width, offset):
        return lax.broadcasted_iota(jnp.int32, (per_wave, width), 1) + offset

    def part_copy(d, lo, width, number):
        peer = (fld + d) % n_fld
        return pltpu.make_async_remote_copy(
            src_ref=part_send.at[peer, :, pl.ds(lo, width)],
            dst_ref=part_recv.at[d - 1, :, pl.ds(lo, width)],
            send_sem=part_send_sem.at[d - 1],
            recv_sem=part_recv_sem.at[d - 1, number],
            device_id=(lat, peer),
            device_id_type=MESH,
        )

    def left_over(pair, start, width):
        first_rows = lax.shift_right_logical(wave_count - owned_ref[first_owned + 2 * pair], 1)
        product = project(operand(rows_anti, pair), start, width)
        degree = degree_index(width, 0) + (wave_count // 2 - 1 - pair)
        return choose(product, degree < first_rows)

    def pair_chunk(c, carry):
        start = pl.multiple_of(c * wave_count, min(wave_count, 1280))
        wave = owned_ref[first_owned + 2 * c]
        first_even = lax.shift_right_logical(wave_count + 1 - wave, 1)
        first_odd = lax.shift_right_logical(wave_count - wave, 1)
        sym = project(operand(rows_sym, c), start, sym_end)
        sym = choose(sym, degree_index(sym_end, -c) < first_even)
        anti_width = wave_count - anti_start
        anti_from = pl.multiple_of(start + anti_start, lane_tile)
        anti = project(operand(rows_anti, c), anti_from, anti_width)
        anti = choose(anti, degree_index(anti_width, anti_start - even - c) < first_odd)
        before = left_over(jnp.maximum(c - 1, 0), start, lane_tile)
        head = jnp.where(degree_index(lane_tile, 0) < c, before, sym[:, :lane_tile])
        middle = jnp.where(
            degree_index(sym_end - anti_start, anti_start - c) < even,
            sym[:, anti_start:],
            anti[:, : sym_end - anti_start],
        )
        pieces = [head, sym[:, lane_tile:anti_start], middle, anti[:, sym_end - anti_start :]]
        at = 0
        for piece in pieces:
            width = piece.shape[1]
            if width == 0:
                continue
            lanes = pl.ds(pl.multiple_of(start + at, lane_tile), width)
            partial[:, lanes] = piece
            for f in range(n_fld):
                part_send[f, :, lanes] = piece[f * kinds : (f + 1) * kinds].astype(jnp.bfloat16)
            at += width
        for d in range(1, n_fld):
            part_copy(d, start, wave_count, c).start()
        return carry

    tail = total - pairs * wave_count
    tail_from = pairs * wave_count
    tail_wide = part_send.shape[2] - tail_from

    mine = pl.multiple_of(fld * kinds, kinds)
    batch_rows = kinds // 2

    def finish(lo, width, kept, number):
        for d in range(1, n_fld):
            part_copy(d, lo, width, number).wait_recv()
        result = partial[pl.ds(mine, kinds), pl.ds(lo, kept)]
        for d in range(1, n_fld):
            result = result + part_recv[d - 1, :, pl.ds(lo, kept)].astype(jnp.float32)
        out_ref[0, :, pl.ds(lo, kept)] = result[:batch_rows]
        out_ref[1, :, pl.ds(lo, kept)] = result[batch_rows:]

    def finish_pair(c, carry):
        start = pl.multiple_of(c * wave_count, min(wave_count, 1280))
        finish(start, wave_count, wave_count, c)
        return carry

    load.wait()
    finished = 0
    for number in range(n_groups):
        gather_group(number)
        first = firsts[number] // 2
        lax.fori_loop(first, first + sizes[number] // 2, pair_chunk, 0)
        if number + 2 < n_groups:
            send(number + 2, number + 1)
        if number == n_groups - 2:
            finished = firsts[max(number - 1, 1)] // 2
            lax.fori_loop(0, finished, finish_pair, 0)

    piece = left_over(pairs - 1, tail_from, tail)
    partial[:, tail_from : tail_from + tail] = piece
    for f in range(n_fld):
        part_send[f, :, tail_from : tail_from + tail] = piece[
            f * kinds : (f + 1) * kinds
        ].astype(jnp.bfloat16)
    for d in range(1, n_fld):
        part_copy(d, tail_from, tail_wide, pairs).start()

    def last_left(batch, carry):
        left(n_groups - 1, batch)
        return carry

    lax.fori_loop(0, batches, last_left, 0)
    lax.fori_loop(finished, pairs, finish_pair, 0)
    finish(tail_from, tail_wide, tail, pairs)
    for d in range(1, n_fld):
        whole = part_send.at[(fld + d) % n_fld]
        pltpu.make_async_copy(whole, whole, part_send_sem.at[d - 1]).wait()


def shards(fourier, legendre, cycle_points, wave_order, lane_tile=256):
    n_lat, n_fld = lax.axis_size("lat"), lax.axis_size("fld")
    batches, rows_each, fields, parts, wave_count = fourier.shape
    kinds = batches * fields * parts
    columns = kinds * rows_each
    owner_waves = wave_count // n_lat
    total, lat_depth = legendre.shape
    depth = n_lat // 2 // n_fld
    slots = 2 * depth * n_fld
    per_wave = n_fld * kinds
    padded = round_up(total, 128)
    tiles = -(-lat_depth // 128)

    sizes = GROUPS
    x = jnp.transpose(fourier, (0, 2, 3, 1, 4)).reshape(columns, wave_count)
    vmem = pl.BlockSpec(memory_space=pltpu.VMEM)
    return pl.pallas_call(
        functools.partial(exchange_kernel, n_lat, n_fld, lane_tile, sizes),
        out_shape=jax.ShapeDtypeStruct((batches, fields * parts, total), jnp.float32),
        in_specs=[
            vmem,
            vmem,
            vmem,
            pl.BlockSpec(memory_space=pltpu.SMEM),
            pl.BlockSpec(memory_space=pltpu.HBM),
        ],
        out_specs=vmem,
        scratch_shapes=[
            *(pltpu.VMEM((n_lat, count, columns), jnp.bfloat16) for count in sizes),
            *(pltpu.VMEM((slots, count, columns), jnp.bfloat16) for count in sizes),
            pltpu.VMEM((round_up(wave_count, 128) + 8, 128), jnp.int32),
            pltpu.VMEM((lat_depth, total), jnp.bfloat16),
            pltpu.VMEM((depth, 8, columns), jnp.float32),
            pltpu.VMEM((depth, 8, columns), jnp.float32),
            pltpu.VMEM((tiles, owner_waves * per_wave, 128), jnp.float32),
            pltpu.VMEM((tiles, owner_waves * per_wave, 128), jnp.float32),
            pltpu.VMEM((per_wave, padded), jnp.float32),
            pltpu.VMEM((n_fld, kinds, padded), jnp.bfloat16),
            pltpu.VMEM((n_fld - 1, kinds, padded), jnp.bfloat16),
            pltpu.SemaphoreType.DMA((len(sizes), n_lat // 8)),
            pltpu.SemaphoreType.DMA((len(sizes), n_fld)),
            pltpu.SemaphoreType.DMA,
            pltpu.SemaphoreType.DMA((n_fld - 1,)),
            pltpu.SemaphoreType.DMA((n_fld - 1, owner_waves // 2 + 1)),
        ],
        compiler_params=pltpu.CompilerParams(
            collective_id=0, has_side_effects=True, vmem_limit_bytes=48 * 2**20
        ),
        cost_estimate=pl.CostEstimate(
            flops=4 * columns * wave_count * wave_count,
            bytes_accessed=total * lat_depth * 2,
            transcendentals=0,
        ),
    )(x, cycle_points, wave_order, wave_order, legendre.T)


def solution(mesh):
    placed = (P(None, "lat", "fld", None, None), P("lat", "fld"), P("lat"), P())
    return jax.shard_map(
        shards, mesh=mesh, in_specs=placed, out_specs=P(None, "fld", "lat"), check_vma=False
    )
```

```python
import functools

import jax
import jax.numpy as jnp
from jax import lax
from jax.experimental import pallas as pl
from jax.experimental.pallas import tpu as pltpu
from jax.sharding import PartitionSpec as P

MESH = pl.DeviceIdType.MESH
NT = (((1,), (1,)), ((), ()))
GROUPS = (4, 4, 4, 4, 4)


def round_up(value, step):
    return -(-value // step) * step


def exchange_kernel(
    n_lat,
    n_fld,
    lane_tile,
    sizes,
    x_ref,
    points_ref,
    waves_ref,
    owned_ref,
    legendre_ref,
    out_ref,
    *scratch,
):
    n_groups = len(sizes)
    send_bufs, scratch = scratch[:n_groups], scratch[n_groups:]
    recv_bufs, scratch = scratch[:n_groups], scratch[n_groups:]
    (
        wave_cols,
        tables,
        mixed_sym,
        mixed_anti,
        rows_sym,
        rows_anti,
        partial,
        part_send,
        part_recv,
        send_sem,
        recv_sem,
        table_sem,
        part_send_sem,
        part_recv_sem,
    ) = scratch
    lat = lax.axis_index("lat")
    fld = lax.axis_index("fld")
    half = n_lat // 2
    depth = half // n_fld
    sources = 2 * depth
    hemi = lat // half
    block = (lat % half) // depth
    place = lat % depth
    columns, wave_count = x_ref.shape
    owner_waves = sum(sizes)
    firsts = [sum(sizes[:number]) for number in range(n_groups)]
    kinds = part_send.shape[1]
    rows_each = columns // kinds
    pairs = owner_waves // 2
    own = block == fld
    lat_depth, total = legendre_ref.shape
    first_owned = lat * owner_waves

    load = pltpu.make_async_copy(legendre_ref, tables, table_sem)
    load.start()

    barrier = pltpu.get_barrier_semaphore()

    def greet(s, carry):
        source_fld = s // sources
        rest = s % sources
        source_lat = (rest // depth) * half + fld * depth + rest % depth
        itself = jnp.logical_and(source_lat == lat, source_fld == fld)

        @pl.when(jnp.logical_not(itself))
        def _():
            pl.semaphore_signal(
                barrier, inc=1, device_id=(source_lat, source_fld), device_id_type=MESH
            )

        return carry

    lax.fori_loop(0, n_fld * sources, greet, 0)
    for d in range(1, n_fld):
        pl.semaphore_signal(
            barrier, inc=1, device_id=(lat, (fld + d) % n_fld), device_id_type=MESH
        )

    slot = fld * sources + hemi * depth + place

    def copy_to(number, batch, owner):
        return pltpu.make_async_remote_copy(
            src_ref=send_bufs[number].at[owner],
            dst_ref=recv_bufs[number].at[slot],
            send_sem=send_sem.at[number, batch],
            recv_sem=recv_sem.at[number, fld],
            device_id=(owner, block),
            device_id_type=MESH,
        )

    for v in range(-(-wave_count // 128)):
        width = min(128, wave_count - 128 * v)
        line = waves_ref[128 * v : 128 * v + width].reshape(1, width)
        wave_cols[128 * v : 128 * v + width] = jnp.broadcast_to(line, (128, width)).T

    wave_cols[wave_count : wave_count + 8] = jnp.full((8, 128), -1, jnp.int32)

    lane = lax.broadcasted_iota(jnp.int32, (n_lat * 8, 128), 1)
    points = points_ref[...].reshape(1, rows_each)
    limit = jnp.minimum(lax.shift_right_logical(points, 1), wave_count)
    limit = jnp.concatenate([limit] * kinds, axis=1)

    def reorder(number):
        first = firsts[number]
        wave = jnp.concatenate(
            [wave_cols[o * owner_waves + first : o * owner_waves + first + 8] for o in range(n_lat)],
            axis=0,
        )
        pieces = []
        for v in range(-(-wave_count // 128)):
            width = min(128, wave_count - 128 * v)
            hit = jnp.where(wave == lane + 128 * v, 1.0, 0.0).astype(jnp.bfloat16)
            pieces.append(hit[:, :width])
        chosen = jnp.concatenate(pieces, axis=1)
        picked = lax.dot_general(
            chosen, x_ref[...], NT, preferred_element_type=jnp.float32
        )
        wide = jnp.concatenate([wave] * (-(-columns // 128)), axis=1)[:, :columns]
        picked = jnp.where(wide < limit, picked, 0.0)
        for o in range(n_lat):
            part = picked[8 * o : 8 * o + sizes[number]]
            send_bufs[number][o] = part.astype(jnp.bfloat16)

    batches = n_lat // 8
    own_batch, own_step = (5, 7) if n_lat == 64 else (0, 0)

    def target(batch, n):
        if n_lat != 64:
            return (lat + batch * 8 + n) % n_lat
        x = (lat // 16 + batch % 4 + n) % 4
        z = (lat // 2 % 8 + (4, 1, 7, 2, 6, 3, 5, 0)[n]) % 8
        return x * 16 + z * 2 + (lat + batch // 4 + n) % 2

    def left(number, batch):
        buf = send_bufs[number]
        less = jnp.logical_and(own, batch == own_batch)

        @pl.when(less)
        def _():
            done = buf.at[pl.ds(0, 7)]
            pltpu.make_async_copy(done, done, send_sem.at[number, batch]).wait()

        @pl.when(jnp.logical_not(less))
        def _():
            done = buf.at[pl.ds(0, 8)]
            pltpu.make_async_copy(done, done, send_sem.at[number, batch]).wait()

    def send(number, after=None):
        def several(batch, carry):
            if after is not None:
                left(after, batch)
            for n in range(8):
                owner = target(batch, n)
                if n != own_step:
                    copy_to(number, batch, owner).start()
                    continue
                itself = jnp.logical_and(own, batch == own_batch)

                @pl.when(itself)
                def _():
                    pltpu.make_async_copy(
                        send_bufs[number].at[owner],
                        recv_bufs[number].at[slot],
                        recv_sem.at[number, fld],
                    ).start()

                @pl.when(jnp.logical_not(itself))
                def _():
                    copy_to(number, batch, owner).start()

            return carry

        lax.fori_loop(0, batches, several, 0)

    for number in range(n_groups):
        reorder(number)
        if number == 0:
            pl.semaphore_wait(barrier, n_lat + n_fld - 1 - own.astype(jnp.int32))
            send(number)
    send(1, 0)

    def gather_group(number):
        count = sizes[number]
        recv_buf = recv_bufs[number]

        side = 8 // count

        def gather_fields(step, carry):
            for j in range(side):
                f = step * side + j
                here = recv_buf.at[pl.ds(f * sources, sources)]
                pltpu.make_async_copy(here, here, recv_sem.at[number, f]).wait()
                lo = j * count
                for a in range(depth):
                    north = recv_buf[f * sources + a].astype(jnp.float32)
                    south = recv_buf[f * sources + depth + a].astype(jnp.float32)
                    mixed_sym[a, lo : lo + count] = north + south
                    mixed_anti[a, lo : lo + count] = north - south
            for mixed, rows in ((mixed_sym, rows_sym), (mixed_anti, rows_anti)):
                for k in range(kinds):
                    lo = k * rows_each
                    joined = jnp.concatenate(
                        [mixed[a, 0 : side * count, lo : lo + rows_each] for a in range(depth)],
                        axis=1,
                    )
                    for j in range(side):
                        start = firsts[number] * n_fld * kinds + (step * side + j) * kinds + k
                        part = joined[j * count : (j + 1) * count]
                        for v in range(-(-lat_depth // 128)):
                            width = min(128, lat_depth - 128 * v)
                            rows[v, pl.ds(start, count, stride=n_fld * kinds), 0:width] = part[
                                :, 128 * v : 128 * v + width
                            ]
            return carry

        lax.fori_loop(0, n_fld // side, gather_fields, 0)

    per_wave = n_fld * kinds
    even = wave_count // 2 + 1
    sym_end = round_up(even + pairs, lane_tile)
    anti_start = even // lane_tile * lane_tile

    def operand(rows, pair):
        start = pl.multiple_of(pair * (2 * per_wave), 2 * per_wave)
        parts = []
        for v in range(-(-lat_depth // 128)):
            width = min(128, lat_depth - 128 * v)
            parts.append(rows[v, pl.ds(start, 2 * per_wave), 0:width])
        return jnp.concatenate(parts, axis=1).astype(jnp.bfloat16)

    def project(left, start, width):
        return jnp.dot(left, tables[:, pl.ds(start, width)], preferred_element_type=jnp.float32)

    def choose(product, first):
        return jnp.where(first, product[:per_wave], product[per_wave:])

    def degree_index(width, offset):
        return lax.broadcasted_iota(jnp.int32, (per_wave, width), 1) + offset

    def part_copy(d, lo, width, number):
        peer = (fld + d) % n_fld
        return pltpu.make_async_remote_copy(
            src_ref=part_send.at[peer, :, pl.ds(lo, width)],
            dst_ref=part_recv.at[d - 1, :, pl.ds(lo, width)],
            send_sem=part_send_sem.at[d - 1],
            recv_sem=part_recv_sem.at[d - 1, number],
            device_id=(lat, peer),
            device_id_type=MESH,
        )

    def left_over(pair, start, width):
        first_rows = lax.shift_right_logical(wave_count - owned_ref[first_owned + 2 * pair], 1)
        product = project(operand(rows_anti, pair), start, width)
        degree = degree_index(width, 0) + (wave_count // 2 - 1 - pair)
        return choose(product, degree < first_rows)

    def pair_chunk(c, carry):
        start = pl.multiple_of(c * wave_count, min(wave_count, 1280))
        wave = owned_ref[first_owned + 2 * c]
        first_even = lax.shift_right_logical(wave_count + 1 - wave, 1)
        first_odd = lax.shift_right_logical(wave_count - wave, 1)
        sym = project(operand(rows_sym, c), start, sym_end)
        sym = choose(sym, degree_index(sym_end, -c) < first_even)
        anti_width = wave_count - anti_start
        anti_from = pl.multiple_of(start + anti_start, lane_tile)
        anti = project(operand(rows_anti, c), anti_from, anti_width)
        anti = choose(anti, degree_index(anti_width, anti_start - even - c) < first_odd)
        before = left_over(jnp.maximum(c - 1, 0), start, lane_tile)
        head = jnp.where(degree_index(lane_tile, 0) < c, before, sym[:, :lane_tile])
        middle = jnp.where(
            degree_index(sym_end - anti_start, anti_start - c) < even,
            sym[:, anti_start:],
            anti[:, : sym_end - anti_start],
        )
        pieces = [head, sym[:, lane_tile:anti_start], middle, anti[:, sym_end - anti_start :]]
        at = 0
        for piece in pieces:
            width = piece.shape[1]
            if width == 0:
                continue
            lanes = pl.ds(pl.multiple_of(start + at, lane_tile), width)
            partial[:, lanes] = piece
            for f in range(n_fld):
                part_send[f, :, lanes] = piece[f * kinds : (f + 1) * kinds].astype(jnp.bfloat16)
            at += width
        for d in range(1, n_fld):
            part_copy(d, start, wave_count, c).start()
        return carry

    tail = total - pairs * wave_count
    tail_from = pairs * wave_count
    tail_wide = part_send.shape[2] - tail_from

    mine = pl.multiple_of(fld * kinds, kinds)
    batch_rows = kinds // 2

    def finish(lo, width, kept, number):
        for d in range(1, n_fld):
            part_copy(d, lo, width, number).wait_recv()
        result = partial[pl.ds(mine, kinds), pl.ds(lo, kept)]
        for d in range(1, n_fld):
            result = result + part_recv[d - 1, :, pl.ds(lo, kept)].astype(jnp.float32)
        out_ref[0, :, pl.ds(lo, kept)] = result[:batch_rows]
        out_ref[1, :, pl.ds(lo, kept)] = result[batch_rows:]

    def finish_pair(c, carry):
        start = pl.multiple_of(c * wave_count, min(wave_count, 1280))
        finish(start, wave_count, wave_count, c)
        return carry

    load.wait()
    finished = 0
    for number in range(n_groups):
        gather_group(number)
        first = firsts[number] // 2
        lax.fori_loop(first, first + sizes[number] // 2, pair_chunk, 0)
        if number + 2 < n_groups:
            send(number + 2, number + 1)
        if number == n_groups - 2:
            finished = firsts[max(number - 1, 1)] // 2
            lax.fori_loop(0, finished, finish_pair, 0)

    piece = left_over(pairs - 1, tail_from, tail)
    partial[:, tail_from : tail_from + tail] = piece
    for f in range(n_fld):
        part_send[f, :, tail_from : tail_from + tail] = piece[
            f * kinds : (f + 1) * kinds
        ].astype(jnp.bfloat16)
    for d in range(1, n_fld):
        part_copy(d, tail_from, tail_wide, pairs).start()

    def last_left(batch, carry):
        left(n_groups - 1, batch)
        return carry

    lax.fori_loop(0, batches, last_left, 0)
    lax.fori_loop(finished, pairs, finish_pair, 0)
    finish(tail_from, tail_wide, tail, pairs)
    for d in range(1, n_fld):
        whole = part_send.at[(fld + d) % n_fld]
        pltpu.make_async_copy(whole, whole, part_send_sem.at[d - 1]).wait()


def shards(fourier, legendre, cycle_points, wave_order, lane_tile=256):
    n_lat, n_fld = lax.axis_size("lat"), lax.axis_size("fld")
    batches, rows_each, fields, parts, wave_count = fourier.shape
    kinds = batches * fields * parts
    columns = kinds * rows_each
    owner_waves = wave_count // n_lat
    total, lat_depth = legendre.shape
    depth = n_lat // 2 // n_fld
    slots = 2 * depth * n_fld
    per_wave = n_fld * kinds
    padded = round_up(total, 128)
    tiles = -(-lat_depth // 128)

    sizes = GROUPS
    x = jnp.transpose(fourier, (0, 2, 3, 1, 4)).reshape(columns, wave_count)
    vmem = pl.BlockSpec(memory_space=pltpu.VMEM)
    return pl.pallas_call(
        functools.partial(exchange_kernel, n_lat, n_fld, lane_tile, sizes),
        out_shape=jax.ShapeDtypeStruct((batches, fields * parts, total), jnp.float32),
        in_specs=[
            vmem,
            vmem,
            vmem,
            pl.BlockSpec(memory_space=pltpu.SMEM),
            pl.BlockSpec(memory_space=pltpu.HBM),
        ],
        out_specs=vmem,
        scratch_shapes=[
            *(pltpu.VMEM((n_lat, count, columns), jnp.bfloat16) for count in sizes),
            *(pltpu.VMEM((slots, count, columns), jnp.bfloat16) for count in sizes),
            pltpu.VMEM((round_up(wave_count, 128) + 8, 128), jnp.int32),
            pltpu.VMEM((lat_depth, total), jnp.bfloat16),
            pltpu.VMEM((depth, 8, columns), jnp.float32),
            pltpu.VMEM((depth, 8, columns), jnp.float32),
            pltpu.VMEM((tiles, owner_waves * per_wave, 128), jnp.float32),
            pltpu.VMEM((tiles, owner_waves * per_wave, 128), jnp.float32),
            pltpu.VMEM((per_wave, padded), jnp.float32),
            pltpu.VMEM((n_fld, kinds, padded), jnp.bfloat16),
            pltpu.VMEM((n_fld - 1, kinds, padded), jnp.bfloat16),
            pltpu.SemaphoreType.DMA((len(sizes), n_lat // 8)),
            pltpu.SemaphoreType.DMA((len(sizes), n_fld)),
            pltpu.SemaphoreType.DMA,
            pltpu.SemaphoreType.DMA((n_fld - 1,)),
            pltpu.SemaphoreType.DMA((n_fld - 1, owner_waves // 2 + 1)),
        ],
        compiler_params=pltpu.CompilerParams(
            collective_id=0, has_side_effects=True, vmem_limit_bytes=48 * 2**20
        ),
        cost_estimate=pl.CostEstimate(
            flops=4 * columns * wave_count * wave_count,
            bytes_accessed=total * lat_depth * 2,
            transcendentals=0,
        ),
    )(x, cycle_points, wave_order, wave_order, legendre.T)


def solution(mesh):
    placed = (P(None, "lat", "fld", None, None), P("lat", "fld"), P("lat"), P())
    return jax.shard_map(
        shards, mesh=mesh, in_specs=placed, out_specs=P(None, "fld", "lat"), check_vma=False
    )
```

```python
import functools

import jax
import jax.numpy as jnp
from jax import lax
from jax.experimental import pallas as pl
from jax.experimental.pallas import tpu as pltpu
from jax.sharding import PartitionSpec as P

MESH = pl.DeviceIdType.MESH
NT = (((1,), (1,)), ((), ()))
GROUPS = (4, 4, 4, 4, 4)


def round_up(value, step):
    return -(-value // step) * step


def exchange_kernel(
    n_lat,
    n_fld,
    lane_tile,
    sizes,
    x_ref,
    points_ref,
    waves_ref,
    owned_ref,
    legendre_ref,
    out_ref,
    *scratch,
):
    n_groups = len(sizes)
    send_bufs, scratch = scratch[:n_groups], scratch[n_groups:]
    recv_bufs, scratch = scratch[:n_groups], scratch[n_groups:]
    (
        wave_cols,
        tables,
        mixed_sym,
        mixed_anti,
        rows_sym,
        rows_anti,
        partial,
        part_send,
        part_recv,
        send_sem,
        recv_sem,
        table_sem,
        part_send_sem,
        part_recv_sem,
    ) = scratch
    lat = lax.axis_index("lat")
    fld = lax.axis_index("fld")
    half = n_lat // 2
    depth = half // n_fld
    sources = 2 * depth
    hemi = lat // half
    block = (lat % half) // depth
    place = lat % depth
    columns, wave_count = x_ref.shape
    owner_waves = sum(sizes)
    firsts = [sum(sizes[:number]) for number in range(n_groups)]
    kinds = part_send.shape[1]
    rows_each = columns // kinds
    pairs = owner_waves // 2
    own = block == fld
    lat_depth, total = legendre_ref.shape
    first_owned = lat * owner_waves

    load = pltpu.make_async_copy(legendre_ref, tables, table_sem)
    load.start()

    barrier = pltpu.get_barrier_semaphore()

    def greet(s, carry):
        source_fld = s // sources
        rest = s % sources
        source_lat = (rest // depth) * half + fld * depth + rest % depth
        itself = jnp.logical_and(source_lat == lat, source_fld == fld)

        @pl.when(jnp.logical_not(itself))
        def _():
            pl.semaphore_signal(
                barrier, inc=1, device_id=(source_lat, source_fld), device_id_type=MESH
            )

        return carry

    lax.fori_loop(0, n_fld * sources, greet, 0)
    for d in range(1, n_fld):
        pl.semaphore_signal(
            barrier, inc=1, device_id=(lat, (fld + d) % n_fld), device_id_type=MESH
        )

    slot = fld * sources + hemi * depth + place

    def copy_to(number, batch, owner):
        return pltpu.make_async_remote_copy(
            src_ref=send_bufs[number].at[owner],
            dst_ref=recv_bufs[number].at[slot],
            send_sem=send_sem.at[number, batch],
            recv_sem=recv_sem.at[number, fld],
            device_id=(owner, block),
            device_id_type=MESH,
        )

    for v in range(-(-wave_count // 128)):
        width = min(128, wave_count - 128 * v)
        line = waves_ref[128 * v : 128 * v + width].reshape(1, width)
        wave_cols[128 * v : 128 * v + width] = jnp.broadcast_to(line, (128, width)).T

    wave_cols[wave_count : wave_count + 8] = jnp.full((8, 128), -1, jnp.int32)

    points = points_ref[...].reshape(1, rows_each)
    limit = jnp.minimum(lax.shift_right_logical(points, 1), wave_count)
    limit = jnp.concatenate([limit] * kinds, axis=1)

    def reorder(number):
        first, count = firsts[number], sizes[number]
        lane = lax.broadcasted_iota(jnp.int32, (n_lat * count, 128), 1)
        wave = jnp.concatenate(
            [
                wave_cols[o * owner_waves + first : o * owner_waves + first + count]
                for o in range(n_lat)
            ],
            axis=0,
        )
        pieces = []
        for v in range(-(-wave_count // 128)):
            width = min(128, wave_count - 128 * v)
            hit = jnp.where(wave == lane + 128 * v, 1.0, 0.0).astype(jnp.bfloat16)
            pieces.append(hit[:, :width])
        chosen = jnp.concatenate(pieces, axis=1)
        picked = lax.dot_general(
            chosen, x_ref[...], NT, preferred_element_type=jnp.float32
        )
        wide = jnp.concatenate([wave] * (-(-columns // 128)), axis=1)[:, :columns]
        picked = jnp.where(wide < limit, picked, 0.0)
        for o in range(n_lat):
            part = picked[count * o : count * (o + 1)]
            send_bufs[number][o] = part.astype(jnp.bfloat16)

    batches = n_lat // 8
    own_batch, own_step = (5, 7) if n_lat == 64 else (0, 0)

    def target(batch, n):
        if n_lat != 64:
            return (lat + batch * 8 + n) % n_lat
        x = (lat // 16 + batch % 4 + n) % 4
        z = (lat // 2 % 8 + (4, 1, 7, 2, 6, 3, 5, 0)[n]) % 8
        return x * 16 + z * 2 + (lat + batch // 4 + n) % 2

    def left(number, batch):
        buf = send_bufs[number]
        less = jnp.logical_and(own, batch == own_batch)

        @pl.when(less)
        def _():
            done = buf.at[pl.ds(0, 7)]
            pltpu.make_async_copy(done, done, send_sem.at[number, batch]).wait()

        @pl.when(jnp.logical_not(less))
        def _():
            done = buf.at[pl.ds(0, 8)]
            pltpu.make_async_copy(done, done, send_sem.at[number, batch]).wait()

    def send(number, after=None):
        def several(batch, carry):
            if after is not None:
                left(after, batch)
            for n in range(8):
                owner = target(batch, n)
                if n != own_step:
                    copy_to(number, batch, owner).start()
                    continue
                itself = jnp.logical_and(own, batch == own_batch)

                @pl.when(itself)
                def _():
                    pltpu.make_async_copy(
                        send_bufs[number].at[owner],
                        recv_bufs[number].at[slot],
                        recv_sem.at[number, fld],
                    ).start()

                @pl.when(jnp.logical_not(itself))
                def _():
                    copy_to(number, batch, owner).start()

            return carry

        lax.fori_loop(0, batches, several, 0)

    for number in range(n_groups):
        reorder(number)
        if number == 0:
            pl.semaphore_wait(barrier, n_lat + n_fld - 1 - own.astype(jnp.int32))
            send(number)
    send(1, 0)

    def gather_group(number):
        count = sizes[number]
        recv_buf = recv_bufs[number]

        side = 8 // count

        def gather_fields(step, carry):
            for j in range(side):
                f = step * side + j
                here = recv_buf.at[pl.ds(f * sources, sources)]
                pltpu.make_async_copy(here, here, recv_sem.at[number, f]).wait()
                lo = j * count
                for a in range(depth):
                    north = recv_buf[f * sources + a].astype(jnp.float32)
                    south = recv_buf[f * sources + depth + a].astype(jnp.float32)
                    mixed_sym[a, lo : lo + count] = north + south
                    mixed_anti[a, lo : lo + count] = north - south
            for mixed, rows in ((mixed_sym, rows_sym), (mixed_anti, rows_anti)):
                for k in range(kinds):
                    lo = k * rows_each
                    joined = jnp.concatenate(
                        [mixed[a, 0 : side * count, lo : lo + rows_each] for a in range(depth)],
                        axis=1,
                    )
                    for j in range(side):
                        start = firsts[number] * n_fld * kinds + (step * side + j) * kinds + k
                        part = joined[j * count : (j + 1) * count]
                        for v in range(-(-lat_depth // 128)):
                            width = min(128, lat_depth - 128 * v)
                            rows[v, pl.ds(start, count, stride=n_fld * kinds), 0:width] = part[
                                :, 128 * v : 128 * v + width
                            ]
            return carry

        lax.fori_loop(0, n_fld // side, gather_fields, 0)

    per_wave = n_fld * kinds
    even = wave_count // 2 + 1
    sym_end = round_up(even + pairs, lane_tile)
    anti_start = even // lane_tile * lane_tile

    def operand(rows, pair):
        start = pl.multiple_of(pair * (2 * per_wave), 2 * per_wave)
        parts = []
        for v in range(-(-lat_depth // 128)):
            width = min(128, lat_depth - 128 * v)
            parts.append(rows[v, pl.ds(start, 2 * per_wave), 0:width])
        return jnp.concatenate(parts, axis=1).astype(jnp.bfloat16)

    def project(left, start, width):
        return jnp.dot(left, tables[:, pl.ds(start, width)], preferred_element_type=jnp.float32)

    def choose(product, first):
        return jnp.where(first, product[:per_wave], product[per_wave:])

    def degree_index(width, offset):
        return lax.broadcasted_iota(jnp.int32, (per_wave, width), 1) + offset

    def part_copy(d, lo, width, number):
        peer = (fld + d) % n_fld
        return pltpu.make_async_remote_copy(
            src_ref=part_send.at[peer, :, pl.ds(lo, width)],
            dst_ref=part_recv.at[d - 1, :, pl.ds(lo, width)],
            send_sem=part_send_sem.at[d - 1],
            recv_sem=part_recv_sem.at[d - 1, number],
            device_id=(lat, peer),
            device_id_type=MESH,
        )

    def left_over(pair, start, width):
        first_rows = lax.shift_right_logical(wave_count - owned_ref[first_owned + 2 * pair], 1)
        product = project(operand(rows_anti, pair), start, width)
        degree = degree_index(width, 0) + (wave_count // 2 - 1 - pair)
        return choose(product, degree < first_rows)

    def pair_chunk(c, carry):
        start = pl.multiple_of(c * wave_count, min(wave_count, 1280))
        wave = owned_ref[first_owned + 2 * c]
        first_even = lax.shift_right_logical(wave_count + 1 - wave, 1)
        first_odd = lax.shift_right_logical(wave_count - wave, 1)
        sym = project(operand(rows_sym, c), start, sym_end)
        sym = choose(sym, degree_index(sym_end, -c) < first_even)
        anti_width = wave_count - anti_start
        anti_from = pl.multiple_of(start + anti_start, lane_tile)
        anti = project(operand(rows_anti, c), anti_from, anti_width)
        anti = choose(anti, degree_index(anti_width, anti_start - even - c) < first_odd)
        before = left_over(jnp.maximum(c - 1, 0), start, lane_tile)
        head = jnp.where(degree_index(lane_tile, 0) < c, before, sym[:, :lane_tile])
        middle = jnp.where(
            degree_index(sym_end - anti_start, anti_start - c) < even,
            sym[:, anti_start:],
            anti[:, : sym_end - anti_start],
        )
        pieces = [head, sym[:, lane_tile:anti_start], middle, anti[:, sym_end - anti_start :]]
        at = 0
        for piece in pieces:
            width = piece.shape[1]
            if width == 0:
                continue
            lanes = pl.ds(pl.multiple_of(start + at, lane_tile), width)
            partial[:, lanes] = piece
            for f in range(n_fld):
                part_send[f, :, lanes] = piece[f * kinds : (f + 1) * kinds].astype(jnp.bfloat16)
            at += width
        for d in range(1, n_fld):
            part_copy(d, start, wave_count, c).start()
        return carry

    tail = total - pairs * wave_count
    tail_from = pairs * wave_count
    tail_wide = part_send.shape[2] - tail_from

    mine = pl.multiple_of(fld * kinds, kinds)
    batch_rows = kinds // 2

    def finish(lo, width, kept, number):
        for d in range(1, n_fld):
            part_copy(d, lo, width, number).wait_recv()
        result = partial[pl.ds(mine, kinds), pl.ds(lo, kept)]
        for d in range(1, n_fld):
            result = result + part_recv[d - 1, :, pl.ds(lo, kept)].astype(jnp.float32)
        out_ref[0, :, pl.ds(lo, kept)] = result[:batch_rows]
        out_ref[1, :, pl.ds(lo, kept)] = result[batch_rows:]

    def finish_pair(c, carry):
        start = pl.multiple_of(c * wave_count, min(wave_count, 1280))
        finish(start, wave_count, wave_count, c)
        return carry

    load.wait()
    def send_tail():
        piece = left_over(pairs - 1, tail_from, tail)
        partial[:, tail_from : tail_from + tail] = piece
        for f in range(n_fld):
            part_send[f, :, tail_from : tail_from + tail] = piece[
                f * kinds : (f + 1) * kinds
            ].astype(jnp.bfloat16)
        for d in range(1, n_fld):
            part_copy(d, tail_from, tail_wide, pairs).start()

    finished = 0
    for number in range(n_groups):
        gather_group(number)
        if number == n_groups - 1:
            send_tail()
        first = firsts[number] // 2
        lax.fori_loop(first, first + sizes[number] // 2, pair_chunk, 0)
        if number + 2 < n_groups:
            send(number + 2, number + 1)
        if number == n_groups - 2:
            finished = firsts[max(number - 1, 1)] // 2
            lax.fori_loop(0, finished, finish_pair, 0)

    def last_left(batch, carry):
        left(n_groups - 1, batch)
        return carry

    lax.fori_loop(0, batches, last_left, 0)
    lax.fori_loop(finished, pairs, finish_pair, 0)
    finish(tail_from, tail_wide, tail, pairs)
    for d in range(1, n_fld):
        whole = part_send.at[(fld + d) % n_fld]
        pltpu.make_async_copy(whole, whole, part_send_sem.at[d - 1]).wait()


def shards(fourier, legendre, cycle_points, wave_order, lane_tile=256):
    n_lat, n_fld = lax.axis_size("lat"), lax.axis_size("fld")
    batches, rows_each, fields, parts, wave_count = fourier.shape
    kinds = batches * fields * parts
    columns = kinds * rows_each
    owner_waves = wave_count // n_lat
    total, lat_depth = legendre.shape
    depth = n_lat // 2 // n_fld
    slots = 2 * depth * n_fld
    per_wave = n_fld * kinds
    padded = round_up(total, 128)
    tiles = -(-lat_depth // 128)

    sizes = GROUPS
    x = jnp.transpose(fourier, (0, 2, 3, 1, 4)).reshape(columns, wave_count)
    vmem = pl.BlockSpec(memory_space=pltpu.VMEM)
    return pl.pallas_call(
        functools.partial(exchange_kernel, n_lat, n_fld, lane_tile, sizes),
        out_shape=jax.ShapeDtypeStruct((batches, fields * parts, total), jnp.float32),
        in_specs=[
            vmem,
            vmem,
            vmem,
            pl.BlockSpec(memory_space=pltpu.SMEM),
            pl.BlockSpec(memory_space=pltpu.HBM),
        ],
        out_specs=vmem,
        scratch_shapes=[
            *(pltpu.VMEM((n_lat, count, columns), jnp.bfloat16) for count in sizes),
            *(pltpu.VMEM((slots, count, columns), jnp.bfloat16) for count in sizes),
            pltpu.VMEM((round_up(wave_count, 128) + 8, 128), jnp.int32),
            pltpu.VMEM((lat_depth, total), jnp.bfloat16),
            pltpu.VMEM((depth, 8, columns), jnp.float32),
            pltpu.VMEM((depth, 8, columns), jnp.float32),
            pltpu.VMEM((tiles, owner_waves * per_wave, 128), jnp.float32),
            pltpu.VMEM((tiles, owner_waves * per_wave, 128), jnp.float32),
            pltpu.VMEM((per_wave, padded), jnp.float32),
            pltpu.VMEM((n_fld, kinds, padded), jnp.bfloat16),
            pltpu.VMEM((n_fld - 1, kinds, padded), jnp.bfloat16),
            pltpu.SemaphoreType.DMA((len(sizes), n_lat // 8)),
            pltpu.SemaphoreType.DMA((len(sizes), n_fld)),
            pltpu.SemaphoreType.DMA,
            pltpu.SemaphoreType.DMA((n_fld - 1,)),
            pltpu.SemaphoreType.DMA((n_fld - 1, owner_waves // 2 + 1)),
        ],
        compiler_params=pltpu.CompilerParams(
            collective_id=0, has_side_effects=True, vmem_limit_bytes=48 * 2**20
        ),
        cost_estimate=pl.CostEstimate(
            flops=4 * columns * wave_count * wave_count,
            bytes_accessed=total * lat_depth * 2,
            transcendentals=0,
        ),
    )(x, cycle_points, wave_order, wave_order, legendre.T)


def solution(mesh):
    placed = (P(None, "lat", "fld", None, None), P("lat", "fld"), P("lat"), P())
    return jax.shard_map(
        shards, mesh=mesh, in_specs=placed, out_specs=P(None, "fld", "lat"), check_vma=False
    )
```
